32 devices in a mesh: dp: 8 (over z, x), cluster: 4 (over y, core).
Axes of the slice: x: 2, y: 2, z: 4, core: 2. Of those that a mesh axis runs over, the one named last changes fastest.
Arguments:
- home_rows: bfloat16 [49152, 768], P(('dp', 'cluster')), may hold values from -6 to 6
- guest_rows: bfloat16 [8192, 768], P(('dp', 'cluster')), may hold values from -6 to 6
- home_cluster: int32 [192], replicated, may hold values from 0 to 7, as said below
- guest_cluster: int32 [32], replicated, may hold values from 0 to 7, as said below
- pair_mask: int32 [32, 6, 8], P(('dp', 'cluster')), may hold values from 0 to 1, as said below
Outputs:
- home_score: float32 [49152], P(('dp', 'cluster'))
- guest_score: float32 [8192], P(('dp', 'cluster'))
The draws below stay inside these ranges and needn't reach their ends.
Inputs may be any that keep to these rules, and one draw needn't show every extreme that they name: `home_cluster`: blocks of the devices at cluster indices 2 g and 2 g + 1 carry ids from g * 4 to (g + 1) * 4 - 1. `guest_cluster`: blocks of the devices at cluster indices 2 g and 2 g + 1 carry ids from g * 4 to (g + 1) * 4 - 1. `pair_mask`: an entry is 1 where the resident block and the visiting block it names carry one cluster id, else 0.
All inputs are finite; a program needn't handle non-finite values.
Results may differ from the reference program's by a relative error of at most 0.0003.
Values may be sent and summed in bfloat16 or wider, within the bound.
A program may use at most 128 MiB of HBM per device.

```python
import jax
import jax.numpy as jnp
import numpy as np
from jax import lax

D = 768
BLOCK = 256
STAT_DEV = 6
CLUSTERS = 4
STAT_ROWS = 49152
GUEST_ROWS = 8192
N_DP = 8
N_CLUSTER = 4


def cluster_tables(key):
    key_home = jax.random.fold_in(key, 11)
    key_guest = jax.random.fold_in(key, 12)
    key_label = jax.random.fold_in(key, 13)
    devices_all = N_DP * N_CLUSTER
    weights = [1000 // (i + 1) for i in range(CLUSTERS)]
    bounds = np.cumsum(np.array(weights, dtype=np.int64))
    overall = int(bounds[-1])
    inner = jnp.asarray(bounds[:-1].astype(np.int32))
    relabel = jax.random.permutation(key_label, CLUSTERS).astype(jnp.int32)
    groups = jnp.arange(devices_all, dtype=jnp.int32) % N_CLUSTER // 2

    def pick_ids(which, slots):
        drawn = jax.random.randint(which, (devices_all, slots), 0, overall, dtype=jnp.int32)
        picked = jnp.sum((drawn[..., None] >= inner).astype(jnp.int32), axis=-1)
        return groups[:, None] * CLUSTERS + relabel[picked]
    home_ids = pick_ids(key_home, STAT_DEV)
    guest_ids = pick_ids(key_guest, 1)[:, 0]
    home_grid = home_ids.reshape(N_DP, N_CLUSTER, STAT_DEV)
    guest_grid = guest_ids.reshape(N_DP, N_CLUSTER)
    mirrored = guest_grid[:, jnp.bitwise_xor(jnp.arange(N_CLUSTER, dtype=jnp.int32), 1)]
    matched = (home_grid[:, :, :, None] == jnp.transpose(mirrored)[None, :, None, :]).astype(jnp.int32)
    return (home_ids.reshape(-1), guest_ids, matched.reshape(devices_all, STAT_DEV, N_DP))


def draw_home_cluster(key, part):
    return cluster_tables(key)[0]


def draw_guest_cluster(key, part):
    return cluster_tables(key)[1]


def draw_pair_mask(key, part):
    return cluster_tables(key)[2]


def block_levels(own_key, extent, shards, low, largest):
    def one(position, blocks):
        steps = jax.random.uniform(jax.random.fold_in(jax.random.fold_in(own_key, 6), position), (blocks,), jnp.float32, low / len(shards), largest / len(shards))
        return jnp.repeat(jnp.exp(steps), extent[position] // blocks).reshape((-1,) + (1,) * (len(extent) - position - 1))

    gain = one(*shards[0])
    for cut in shards[1:]:
        gain = gain * one(*cut)
    return gain


def bell_draw(stream_key, shape, spread, bound, split=(), kind=jnp.bfloat16):
    result = jax.random.normal(stream_key, shape, jnp.float32) * spread
    if len(split) > 0:
        result = block_levels(stream_key, shape, split, -0.22, 0.18) * result
    return jnp.clip(result, min=-bound, max=bound).astype(kind)


def setup_inputs(seed: int = 0) -> dict:
    arg_keys = jax.random.split(jax.random.key(seed), 6)
    home_rows = bell_draw(arg_keys[0], (STAT_ROWS, D), 1.0, 6.0, ((0, 32),))
    guest_rows = bell_draw(arg_keys[1], (GUEST_ROWS, D), 1.0, 6.0, ((0, 32),))
    home_cluster = draw_home_cluster(jax.random.fold_in(arg_keys[5], 71), 0)
    guest_cluster = draw_guest_cluster(jax.random.fold_in(arg_keys[5], 71), 0)
    pair_mask = draw_pair_mask(jax.random.fold_in(arg_keys[5], 71), 0)
    return {"home_rows": home_rows, "guest_rows": guest_rows, "home_cluster": home_cluster, "guest_cluster": guest_cluster, "pair_mask": pair_mask}


SHARPNESS = 30.0
EPSILON = 1e-06

def reference(home_rows, guest_rows, home_cluster, guest_cluster, pair_mask):
    devices_all = N_DP * N_CLUSTER
    resident = home_rows.reshape(devices_all * STAT_DEV, BLOCK, D)
    visiting = guest_rows.reshape(N_DP, N_CLUSTER, BLOCK, D)
    res_f = resident.astype(jnp.float32)
    inv_resident = 1.0 / jnp.sqrt(lax.optimization_barrier(jnp.sum(res_f * res_f, axis=-1)) + EPSILON)
    vis_f = visiting.astype(jnp.float32)
    inv_visiting = 1.0 / jnp.sqrt(lax.optimization_barrier(jnp.sum(vis_f * vis_f, axis=-1)) + EPSILON)
    listed_all = pair_mask.reshape(devices_all * STAT_DEV, N_DP).astype(jnp.float32)

    def one_block(guest_acc, number):
        device = number // STAT_DEV
        column = device % N_CLUSTER
        partner = jnp.bitwise_xor(column, 1).astype(jnp.int32)
        partners = lax.dynamic_index_in_dim(visiting, partner, 1, keepdims=False).reshape(N_DP * BLOCK, D)
        inv_partner = lax.dynamic_index_in_dim(inv_visiting, partner, 1, keepdims=False).reshape(N_DP * BLOCK)
        block_rows = resident[number]
        products = jnp.dot(block_rows, partners.T, preferred_element_type=jnp.float32)
        cosine = products * inv_resident[number][:, None] * inv_partner[None, :]
        weights = jnp.repeat(listed_all[number], BLOCK)
        kernel_tile = jnp.exp(SHARPNESS * cosine) * weights[None, :]
        row_part = lax.optimization_barrier(jnp.sum(kernel_tile, axis=1))
        col_part = lax.optimization_barrier(jnp.sum(kernel_tile, axis=0)).reshape(N_DP, BLOCK)
        guest_acc = guest_acc.at[:, partner].add(col_part)
        return (guest_acc, row_part)
    start_acc = jnp.zeros((N_DP, N_CLUSTER, BLOCK), jnp.float32)
    guest_acc, home_density = lax.scan(one_block, start_acc, jnp.arange(devices_all * STAT_DEV, dtype=jnp.int32))
    id_range = jnp.arange(N_CLUSTER // 2 * CLUSTERS, dtype=jnp.int32)
    members = lax.optimization_barrier(jnp.sum((home_cluster[:, None] == id_range[None, :]).astype(jnp.int32), axis=0))
    members = members + lax.optimization_barrier(jnp.sum((guest_cluster[:, None] == id_range[None, :]).astype(jnp.int32), axis=0))
    home_members = jnp.take(members, home_cluster).astype(jnp.float32)
    guest_members = jnp.take(members, guest_cluster).astype(jnp.float32)
    home_score = jnp.log(1.0 + home_density) - jnp.log(home_members)[:, None]
    guest_density = guest_acc.reshape(devices_all, BLOCK)
    guest_score = jnp.log(1.0 + guest_density) - jnp.log(guest_members)[:, None]
    return (home_score.reshape(-1), guest_score.reshape(-1))
```

```python
import functools

import jax
import jax.numpy as jnp
from jax import lax
from jax.experimental import pallas as pl
from jax.experimental.pallas import tpu as pltpu
from jax.sharding import PartitionSpec as P

BLOCK = 256
PARTS = 2
CHUNK = BLOCK // PARTS

SHARPNESS = 30.0
LOG2_E = 1.4426950408889634
EPSILON = 1e-06
MESH = pl.DeviceIdType.MESH


def lane_fold(value):
    return jnp.sum(value.reshape(value.shape[0] // 8, 8, value.shape[1]), axis=0)


def kernel(
    ndp, slots, home_ref, guest_ref, home_ids, guest_ids, mask_ref, home_out, guest_out,
    rows, turned, blocks, inv_home, home_acc, col_parts, inbox,
    load_sem, own_sem, line_sem, side_sem, recv_sem, col_send, col_recv,
):
    d = lax.axis_index("dp")
    c = lax.axis_index("cluster")
    n_cluster = lax.axis_size("cluster")
    count = ndp // 2
    z = lax.div(d, 2)
    x = lax.rem(d, 2)
    mirror = c + 1 - 2 * lax.rem(c, 2)
    beside = d + 1 - 2 * x
    has_up = z < count - 1
    has_down = z > 0

    load = pltpu.make_async_copy(home_ref, rows, load_sem)
    load.start()

    barrier = pltpu.get_barrier_semaphore()

    def greet(dp, cluster):
        pl.semaphore_signal(barrier, inc=1, device_id=(dp, cluster), device_id_type=MESH)

    greet(d, mirror)
    for column in (c, mirror):
        greet(beside, column)

        @pl.when(has_up)
        def _():
            greet(d + 2, column)

        @pl.when(has_down)
        def _():
            greet(d - 2, column)

    pl.semaphore_wait(barrier, 3 + 2 * has_up.astype(jnp.int32) + 2 * has_down.astype(jnp.int32))

    def own_copy(part, way, target):
        return pltpu.make_async_remote_copy(
            src_ref=guest_ref.at[pl.ds(part * CHUNK, CHUNK), :],
            dst_ref=blocks.at[d, part],
            send_sem=own_sem.at[way, part],
            recv_sem=recv_sem.at[d, part],
            device_id=(target, mirror),
            device_id_type=MESH,
        )

    def own_each(act):
        for part in range(PARTS):

            @pl.when(has_up)
            def _():
                act(own_copy(part, 0, d + 2))

            @pl.when(has_down)
            def _():
                act(own_copy(part, 1, d - 2))

            act(own_copy(part, 2, beside))
            act(own_copy(part, 3, d))

    own_each(lambda copy: copy.start())

    def passed(slot, part, sem, target):
        return pltpu.make_async_remote_copy(
            src_ref=blocks.at[slot, part],
            dst_ref=blocks.at[slot, part],
            send_sem=sem.at[slot, part],
            recv_sem=recv_sem.at[slot, part],
            device_id=(target, c),
            device_id_type=MESH,
        )

    def pass_each(zz, xx, part, act):
        slot = zz * 2 + xx
        on_line = xx == x
        last = part == PARTS - 1
        low = jnp.logical_and(last, zz == 0)
        high = jnp.logical_and(last, zz == count - 1)
        off_line = jnp.logical_not(on_line)
        go_up = jnp.logical_or(
            jnp.logical_and(on_line, zz < z), jnp.logical_and(off_line, low)
        )
        go_down = jnp.logical_or(
            jnp.logical_and(on_line, zz > z), jnp.logical_and(off_line, high)
        )
        go_side = jnp.logical_and(
            jnp.logical_and(on_line, zz != z), jnp.logical_not(jnp.logical_or(low, high))
        )

        @pl.when(jnp.logical_and(has_up, go_up))
        def _():
            act(passed(slot, part, line_sem, d + 2))

        @pl.when(jnp.logical_and(has_down, go_down))
        def _():
            act(passed(slot, part, line_sem, d - 2))

        @pl.when(go_side)
        def _():
            act(passed(slot, part, side_sem, beside))

    def col_copy(slot):
        return pltpu.make_async_remote_copy(
            src_ref=col_parts.at[slot],
            dst_ref=inbox.at[d],
            send_sem=col_send.at[slot],
            recv_sem=col_recv.at[d],
            device_id=(slot, mirror),
            device_id_type=MESH,
        )

    load.wait()

    def prepare(slot, carry):
        own = rows[pl.ds(pl.multiple_of(slot * BLOCK, BLOCK), BLOCK), :]
        flipped = own.T
        turned[slot] = flipped
        values = flipped.astype(jnp.float32)
        total = jnp.sum(lane_fold(values * values), axis=0, keepdims=True)
        scale = (SHARPNESS * LOG2_E) / jnp.sqrt(total + EPSILON)
        inv_home[slot] = jnp.broadcast_to(scale, (8, BLOCK))
        home_acc[slot] = jnp.zeros((8, BLOCK), jnp.float32)
        return carry

    lax.fori_loop(0, slots, prepare, 0)

    device = d * n_cluster + c
    wanted = [home_ids[device * slots + s] for s in range(slots)] + [guest_ids[device]]

    def counted(ids):
        def step(i, totals):
            value = ids[i]
            return tuple(t + (value == w).astype(jnp.int32) for t, w in zip(totals, wanted))

        return step

    members = tuple(jnp.int32(0) for _ in wanted)
    members = lax.fori_loop(0, home_ids.shape[0], counted(home_ids), members)
    members = lax.fori_loop(0, guest_ids.shape[0], counted(guest_ids), members)

    def compute(slot, part):
        visitor = blocks[slot, part]
        values = visitor.astype(jnp.float32)
        inv = 1.0 / jnp.sqrt(jnp.sum(values * values, axis=1, keepdims=True) + EPSILON)
        guest_acc = jnp.zeros((CHUNK, 128), jnp.float32)
        for s in range(slots):
            products = jnp.dot(visitor, turned[s], preferred_element_type=jnp.float32)
            tile = jnp.exp2(products * inv * inv_home[s, 0:1, :])
            listed = mask_ref[0, s, slot].astype(jnp.float32)
            home_acc[s] += lane_fold(tile) * listed
            guest_acc += (tile[:, :128] + tile[:, 128:]) * listed
        col_parts[slot, part] = lane_fold(guest_acc.T)

    def item(t, carry):
        k = lax.div(t, 4 * PARTS)
        r = lax.rem(t, 4 * PARTS)
        part = lax.div(r, 4)
        side = lax.div(lax.rem(r, 4), 2)
        plus = lax.rem(r, 2)
        dist = k - side
        zz = z + (2 * plus - 1) * dist
        xx = x + side * (1 - 2 * x)
        valid = (dist >= 0) & (dist < count) & (zz >= 0) & (zz < count)
        valid = valid & jnp.logical_not((dist == 0) & (plus == 1))

        @pl.when(valid)
        def _():
            slot = zz * 2 + xx
            passed(slot, part, line_sem, d).wait_recv()
            pass_each(zz, xx, part, lambda copy: copy.start())
            compute(slot, part)

            @pl.when(part == PARTS - 1)
            def _():
                col_copy(slot).start()

        return carry

    lax.fori_loop(0, (count + 1) * 4 * PARTS, item, 0)

    for s in range(slots):
        density = jnp.sum(home_acc[s], axis=0, keepdims=True)
        number = jnp.full((1, BLOCK), members[s], jnp.int32).astype(jnp.float32)
        home_out[s : s + 1, :] = jnp.log(1.0 + density) - jnp.log(number)

    own_each(lambda copy: copy.wait_send())

    def drain(t, carry):
        slot = lax.div(t, PARTS)
        part = lax.rem(t, PARTS)
        pass_each(lax.div(slot, 2), lax.rem(slot, 2), part, lambda copy: copy.wait_send())
        return carry

    lax.fori_loop(0, ndp * PARTS, drain, 0)

    def collect(t, total):
        pltpu.make_async_remote_copy(
            src_ref=col_parts.at[t],
            dst_ref=inbox.at[t],
            send_sem=col_send.at[t],
            recv_sem=col_recv.at[t],
            device_id=(t, mirror),
            device_id_type=MESH,
        ).wait_recv()
        return total + inbox[t]

    total = lax.fori_loop(0, ndp, collect, jnp.zeros((PARTS, 8, CHUNK), jnp.float32))
    number = jnp.full((1, CHUNK), members[slots], jnp.int32).astype(jnp.float32)
    for part in range(PARTS):
        density = jnp.sum(total[part], axis=0, keepdims=True)
        score = jnp.log(1.0 + density) - jnp.log(number)
        guest_out[:, part * CHUNK : (part + 1) * CHUNK] = score

    def col_drain(t, carry):
        col_copy(t).wait_send()
        return carry

    lax.fori_loop(0, ndp, col_drain, 0)


def body(home_rows, guest_rows, home_cluster, guest_cluster, pair_mask):
    slots = home_rows.shape[0] // BLOCK
    width = home_rows.shape[1]
    ndp = lax.axis_size("dp")
    hbm = pl.BlockSpec(memory_space=pl.ANY)
    smem = pl.BlockSpec(memory_space=pltpu.SMEM)
    vmem = pl.BlockSpec(memory_space=pltpu.VMEM)
    pairs = slots * ndp * BLOCK * BLOCK
    home_score, guest_score = pl.pallas_call(
        functools.partial(kernel, ndp, slots),
        out_shape=(
            jax.ShapeDtypeStruct((slots, BLOCK), jnp.float32),
            jax.ShapeDtypeStruct((1, BLOCK), jnp.float32),
        ),
        in_specs=[hbm, hbm, smem, smem, smem],
        out_specs=(vmem, vmem),
        scratch_shapes=[
            pltpu.VMEM((slots * BLOCK, width), jnp.bfloat16),
            pltpu.VMEM((slots, width, BLOCK), jnp.bfloat16),
            pltpu.VMEM((ndp, PARTS, CHUNK, width), jnp.bfloat16),
            pltpu.VMEM((slots, 8, BLOCK), jnp.float32),
            pltpu.VMEM((slots, 8, BLOCK), jnp.float32),
            pltpu.VMEM((ndp, PARTS, 8, CHUNK), jnp.float32),
            pltpu.VMEM((ndp, PARTS, 8, CHUNK), jnp.float32),
            pltpu.SemaphoreType.DMA,
            pltpu.SemaphoreType.DMA((4, PARTS)),
            pltpu.SemaphoreType.DMA((ndp, PARTS)),
            pltpu.SemaphoreType.DMA((ndp, PARTS)),
            pltpu.SemaphoreType.DMA((ndp, PARTS)),
            pltpu.SemaphoreType.DMA((ndp,)),
            pltpu.SemaphoreType.DMA((ndp,)),
        ],
        compiler_params=pltpu.CompilerParams(
            collective_id=0, has_side_effects=True, vmem_limit_bytes=48 * 2**20
        ),
        cost_estimate=pl.CostEstimate(
            flops=2 * pairs * width,
            bytes_accessed=2 * (home_rows.size + ndp * BLOCK * width),
            transcendentals=pairs,
        ),
    )(home_rows, guest_rows, home_cluster, guest_cluster, pair_mask)
    return (home_score.reshape(-1), guest_score.reshape(-1))


def solution(mesh):
    placed = (
        P(("dp", "cluster"), None),
        P(("dp", "cluster"), None),
        P(),
        P(),
        P(("dp", "cluster"), None, None),
    )
    return jax.shard_map(
        body,
        mesh=mesh,
        in_specs=placed,
        out_specs=(P(("dp", "cluster")), P(("dp", "cluster"))),
        check_vma=False,
    )
```

```python
import functools

import jax
import jax.numpy as jnp
from jax import lax
from jax.experimental import pallas as pl
from jax.experimental.pallas import tpu as pltpu
from jax.sharding import PartitionSpec as P

BLOCK = 256
PARTS = 2
CHUNK = BLOCK // PARTS

SHARPNESS = 30.0
LOG2_E = 1.4426950408889634
EPSILON = 1e-06
MESH = pl.DeviceIdType.MESH


def lane_fold(value):
    return jnp.sum(value.reshape(value.shape[0] // 8, 8, value.shape[1]), axis=0)


def kernel(
    ndp, slots, home_ref, guest_ref, home_hbm, guest_hbm, mask_hbm, home_out, guest_out,
    rows, turned, blocks, inv_home, home_acc, col_parts, inbox, home_ids, guest_ids, mask,
    load_sem, own_sem, line_sem, side_sem, recv_sem, col_send, col_recv,
):
    d = lax.axis_index("dp")
    c = lax.axis_index("cluster")
    n_cluster = lax.axis_size("cluster")
    count = ndp // 2
    z = lax.div(d, 2)
    x = lax.rem(d, 2)
    mirror = c + 1 - 2 * lax.rem(c, 2)
    beside = d + 1 - 2 * x
    has_up = z < count - 1
    has_down = z > 0

    barrier = pltpu.get_barrier_semaphore()

    def greet(dp, cluster):
        pl.semaphore_signal(barrier, inc=1, device_id=(dp, cluster), device_id_type=MESH)

    greet(d, mirror)
    for column in (c, mirror):
        greet(beside, column)

        @pl.when(has_up)
        def _():
            greet(d + 2, column)

        @pl.when(has_down)
        def _():
            greet(d - 2, column)

    loads = [
        pltpu.make_async_copy(source, target, load_sem.at[i])
        for i, (source, target) in enumerate(
            ((home_ref, rows), (home_hbm, home_ids), (guest_hbm, guest_ids), (mask_hbm, mask))
        )
    ]
    for load in loads:
        load.start()

    pl.semaphore_wait(barrier, 3 + 2 * has_up.astype(jnp.int32) + 2 * has_down.astype(jnp.int32))

    def piece(part):
        return pl.ds(part * CHUNK, CHUNK)

    def own_copy(part, way, target):
        return pltpu.make_async_remote_copy(
            src_ref=guest_ref.at[piece(part), :],
            dst_ref=blocks.at[d, piece(part), :],
            send_sem=own_sem.at[way, part],
            recv_sem=recv_sem.at[d, part],
            device_id=(target, mirror),
            device_id_type=MESH,
        )

    def own_each(act):
        for part in range(PARTS):

            @pl.when(has_up)
            def _():
                act(own_copy(part, 0, d + 2))

            @pl.when(has_down)
            def _():
                act(own_copy(part, 1, d - 2))

            act(own_copy(part, 2, beside))
            act(own_copy(part, 3, d))

    own_each(lambda copy: copy.start())

    def passed(slot, part, sem, target):
        return pltpu.make_async_remote_copy(
            src_ref=blocks.at[slot, piece(part), :],
            dst_ref=blocks.at[slot, piece(part), :],
            send_sem=sem.at[slot, part],
            recv_sem=recv_sem.at[slot, part],
            device_id=(target, c),
            device_id_type=MESH,
        )

    def is_end(zz):
        return jnp.logical_or(zz == 0, zz == count - 1)

    def line_each(zz, part, act):
        slot = zz * 2 + x

        @pl.when(jnp.logical_and(has_up, zz < z))
        def _():
            act(passed(slot, part, line_sem, d + 2))

        @pl.when(jnp.logical_and(has_down, zz > z))
        def _():
            act(passed(slot, part, line_sem, d - 2))

        by_side = zz != z
        if part == PARTS - 1:
            by_side = jnp.logical_and(by_side, jnp.logical_not(is_end(zz)))

        @pl.when(by_side)
        def _():
            act(passed(slot, part, side_sem, beside))

    def end_each(zz, act):
        slot = zz * 2 + 1 - x

        @pl.when(jnp.logical_and(has_up, zz == 0))
        def _():
            act(passed(slot, PARTS - 1, line_sem, d + 2))

        @pl.when(jnp.logical_and(has_down, zz == count - 1))
        def _():
            act(passed(slot, PARTS - 1, line_sem, d - 2))

    def col_copy(slot):
        return pltpu.make_async_remote_copy(
            src_ref=col_parts.at[slot],
            dst_ref=inbox.at[d],
            send_sem=col_send.at[slot],
            recv_sem=col_recv.at[d],
            device_id=(slot, mirror),
            device_id_type=MESH,
        )

    for load in loads:
        load.wait()

    def prepare(slot, carry):
        own = rows[pl.ds(pl.multiple_of(slot * BLOCK, BLOCK), BLOCK), :]
        flipped = own.T
        turned[slot] = flipped
        values = flipped.astype(jnp.float32)
        total = jnp.sum(lane_fold(values * values), axis=0, keepdims=True)
        scale = (SHARPNESS * LOG2_E) / jnp.sqrt(total + EPSILON)
        inv_home[slot] = jnp.broadcast_to(scale, (8, BLOCK))
        home_acc[slot] = jnp.zeros((8, BLOCK), jnp.float32)
        return carry

    lax.fori_loop(0, slots, prepare, 0)

    def compute(slot):
        visitor = blocks[slot]
        values = visitor.astype(jnp.float32)
        inv = 1.0 / jnp.sqrt(jnp.sum(values * values, axis=1, keepdims=True) + EPSILON)
        guest_acc = jnp.zeros((BLOCK, 128), jnp.float32)
        for s in range(slots):
            products = jnp.dot(visitor, turned[s], preferred_element_type=jnp.float32)
            tile = jnp.exp2(products * inv * inv_home[s, 0:1, :])
            listed = mask[s, 0, slot].astype(jnp.float32)
            home_acc[s] += lane_fold(tile) * listed
            guest_acc += (tile[:, :128] + tile[:, 128:]) * listed
        col_parts[slot] = lane_fold(guest_acc.T)
        col_copy(slot).start()

    def both_ways(dist, act):
        def way(plus, carry):
            zz = z + (2 * plus - 1) * dist
            valid = (dist >= 0) & (zz >= 0) & (zz < count)
            valid = valid & jnp.logical_not((dist == 0) & (plus == 1))

            @pl.when(valid)
            def _():
                act(zz)

            return carry

        lax.fori_loop(0, 2, way, 0)

    def arrive(zz, xx, part):
        passed(zz * 2 + xx, part, line_sem, d).wait_recv()

    def line_part(part):
        def act(zz):
            arrive(zz, x, part)
            line_each(zz, part, lambda copy: copy.start())

        return act

    def end_part(zz):
        @pl.when(is_end(zz))
        def _():
            arrive(zz, 1 - x, PARTS - 1)
            end_each(zz, lambda copy: copy.start())

    def side_compute(zz):
        for part in range(PARTS - 1):
            arrive(zz, 1 - x, part)

        @pl.when(jnp.logical_not(is_end(zz)))
        def _():
            arrive(zz, 1 - x, PARTS - 1)

        compute(zz * 2 + 1 - x)

    def step(k, carry):
        for part in range(PARTS - 1):
            both_ways(k, line_part(part))
        both_ways(k - 2, side_compute)
        both_ways(k, line_part(PARTS - 1))
        both_ways(k, lambda zz: compute(zz * 2 + x))
        both_ways(k - 1, end_part)
        return carry

    lax.fori_loop(0, count + 2, step, 0)

    device = d * n_cluster + c
    home_list = home_ids[...]
    guest_list = guest_ids[...]

    def pick(ids, place):
        here = lax.broadcasted_iota(jnp.int32, ids.shape, 1) == place
        return jnp.sum(jnp.where(here, ids, 0), axis=1, keepdims=True)

    def log_members(own_id):
        number = jnp.sum((home_list == own_id).astype(jnp.int32), axis=1, keepdims=True)
        number += jnp.sum((guest_list == own_id).astype(jnp.int32), axis=1, keepdims=True)
        return jnp.log(number.astype(jnp.float32))

    for s in range(slots):
        density = jnp.sum(home_acc[s], axis=0, keepdims=True)
        score = jnp.log(1.0 + density) - log_members(pick(home_list, device * slots + s))
        home_out[:, s * BLOCK : (s + 1) * BLOCK] = score
    log_guest = log_members(pick(guest_list, device))

    own_each(lambda copy: copy.wait_send())

    def drain(t, carry):
        for part in range(PARTS):
            line_each(t, part, lambda copy: copy.wait_send())
        end_each(t, lambda copy: copy.wait_send())
        return carry

    lax.fori_loop(0, count, drain, 0)

    def collect(t, total):
        pltpu.make_async_remote_copy(
            src_ref=col_parts.at[t],
            dst_ref=inbox.at[t],
            send_sem=col_send.at[t],
            recv_sem=col_recv.at[t],
            device_id=(t, mirror),
            device_id_type=MESH,
        ).wait_recv()
        return total + inbox[t]

    total = lax.fori_loop(0, ndp, collect, jnp.zeros((8, BLOCK), jnp.float32))
    guest_out[...] = jnp.log(1.0 + jnp.sum(total, axis=0, keepdims=True)) - log_guest

    def col_drain(t, carry):
        col_copy(t).wait_send()
        return carry

    lax.fori_loop(0, ndp, col_drain, 0)


def body(home_rows, guest_rows, home_cluster, guest_cluster, pair_mask):
    slots = home_rows.shape[0] // BLOCK
    width = home_rows.shape[1]
    ndp = lax.axis_size("dp")
    hbm = pl.BlockSpec(memory_space=pltpu.HBM)
    vmem = pl.BlockSpec(memory_space=pltpu.VMEM)
    pairs = slots * ndp * BLOCK * BLOCK
    home_score, guest_score = pl.pallas_call(
        functools.partial(kernel, ndp, slots),
        out_shape=(
            jax.ShapeDtypeStruct((1, slots * BLOCK), jnp.float32),
            jax.ShapeDtypeStruct((1, BLOCK), jnp.float32),
        ),
        in_specs=[hbm] * 5,
        out_specs=(vmem, vmem),
        scratch_shapes=[
            pltpu.VMEM((slots * BLOCK, width), jnp.bfloat16),
            pltpu.VMEM((slots, width, BLOCK), jnp.bfloat16),
            pltpu.VMEM((ndp, BLOCK, width), jnp.bfloat16),
            pltpu.VMEM((slots, 8, BLOCK), jnp.float32),
            pltpu.VMEM((slots, 8, BLOCK), jnp.float32),
            pltpu.VMEM((ndp, 8, BLOCK), jnp.float32),
            pltpu.VMEM((ndp, 8, BLOCK), jnp.float32),
            pltpu.VMEM((1, home_cluster.shape[0]), jnp.int32),
            pltpu.VMEM((1, guest_cluster.shape[0]), jnp.int32),
            pltpu.SMEM((slots, 1, ndp), jnp.int32),
            pltpu.SemaphoreType.DMA((4,)),
            pltpu.SemaphoreType.DMA((4, PARTS)),
            pltpu.SemaphoreType.DMA((ndp, PARTS)),
            pltpu.SemaphoreType.DMA((ndp, PARTS)),
            pltpu.SemaphoreType.DMA((ndp, PARTS)),
            pltpu.SemaphoreType.DMA((ndp,)),
            pltpu.SemaphoreType.DMA((ndp,)),
        ],
        compiler_params=pltpu.CompilerParams(
            collective_id=0, has_side_effects=True, vmem_limit_bytes=64 * 2**20
        ),
        cost_estimate=pl.CostEstimate(
            flops=2 * pairs * width,
            bytes_accessed=2 * (home_rows.size + ndp * BLOCK * width),
            transcendentals=pairs,
        ),
    )(
        home_rows,
        guest_rows,
        home_cluster.reshape(1, -1),
        guest_cluster.reshape(1, -1),
        pair_mask.transpose(1, 0, 2),
    )
    return (home_score.reshape(-1), guest_score.reshape(-1))


def solution(mesh):
    placed = (
        P(("dp", "cluster"), None),
        P(("dp", "cluster"), None),
        P(),
        P(),
        P(("dp", "cluster"), None, None),
    )
    return jax.shard_map(
        body,
        mesh=mesh,
        in_specs=placed,
        out_specs=(P(("dp", "cluster")), P(("dp", "cluster"))),
        check_vma=False,
    )
```

```python
import functools

import jax
import jax.numpy as jnp
from jax import lax
from jax.experimental import pallas as pl
from jax.experimental.pallas import tpu as pltpu
from jax.sharding import PartitionSpec as P

BLOCK = 256
PARTS = 4
CHUNK = BLOCK // PARTS

SHARPNESS = 30.0
LOG2_E = 1.4426950408889634
EPSILON = 1e-06
MESH = pl.DeviceIdType.MESH


def lane_fold(value):
    return jnp.sum(value.reshape(value.shape[0] // 8, 8, value.shape[1]), axis=0)


def kernel(
    ndp, slots, home_ref, guest_ref, home_hbm, guest_hbm, mask_hbm, home_out, guest_out,
    rows, turned, blocks, inv_home, home_acc, col_parts, inbox, home_ids, guest_ids, mask,
    load_sem, own_sem, line_sem, side_sem, recv_sem, col_send, col_recv,
):
    d = lax.axis_index("dp")
    c = lax.axis_index("cluster")
    n_cluster = lax.axis_size("cluster")
    count = ndp // 2
    z = lax.div(d, 2)
    x = lax.rem(d, 2)
    mirror = c + 1 - 2 * lax.rem(c, 2)
    beside = d + 1 - 2 * x
    has_up = z < count - 1
    has_down = z > 0

    barrier = pltpu.get_barrier_semaphore()

    def greet(dp, cluster):
        pl.semaphore_signal(barrier, inc=1, device_id=(dp, cluster), device_id_type=MESH)

    greet(d, mirror)
    for column in (c, mirror):
        greet(beside, column)

        @pl.when(has_up)
        def _():
            greet(d + 2, column)

        @pl.when(has_down)
        def _():
            greet(d - 2, column)

    loads = [
        pltpu.make_async_copy(source, target, load_sem.at[i])
        for i, (source, target) in enumerate(
            ((home_ref, rows), (home_hbm, home_ids), (guest_hbm, guest_ids), (mask_hbm, mask))
        )
    ]
    for load in loads:
        load.start()

    pl.semaphore_wait(barrier, 3 + 2 * has_up.astype(jnp.int32) + 2 * has_down.astype(jnp.int32))

    def piece(part):
        return pl.ds(part * CHUNK, CHUNK)

    def own_copy(part, way, target):
        return pltpu.make_async_remote_copy(
            src_ref=guest_ref.at[piece(part), :],
            dst_ref=blocks.at[d, piece(part), :],
            send_sem=own_sem.at[way, part],
            recv_sem=recv_sem.at[d, part],
            device_id=(target, mirror),
            device_id_type=MESH,
        )

    def own_each(act, parts):
        for part in parts:

            @pl.when(has_up)
            def _():
                act(own_copy(part, 0, d + 2))

            @pl.when(has_down)
            def _():
                act(own_copy(part, 1, d - 2))

            act(own_copy(part, 2, beside))
            act(own_copy(part, 3, d))

    own_each(lambda copy: copy.start(), range(PARTS // 2))

    def passed(slot, part, sem, target):
        return pltpu.make_async_remote_copy(
            src_ref=blocks.at[slot, piece(part), :],
            dst_ref=blocks.at[slot, piece(part), :],
            send_sem=sem.at[slot, part],
            recv_sem=recv_sem.at[slot, part],
            device_id=(target, c),
            device_id_type=MESH,
        )

    def is_end(zz):
        return jnp.logical_or(zz == 0, zz == count - 1)

    def line_each(zz, part, act):
        slot = zz * 2 + x

        @pl.when(jnp.logical_and(has_up, zz < z))
        def _():
            act(passed(slot, part, line_sem, d + 2))

        @pl.when(jnp.logical_and(has_down, zz > z))
        def _():
            act(passed(slot, part, line_sem, d - 2))

        by_side = zz != z
        if part >= PARTS // 2:
            by_side = jnp.logical_and(by_side, jnp.logical_not(is_end(zz)))

        @pl.when(by_side)
        def _():
            act(passed(slot, part, side_sem, beside))

    def end_each(zz, part, act):
        slot = zz * 2 + 1 - x

        @pl.when(jnp.logical_and(has_up, zz == 0))
        def _():
            act(passed(slot, part, line_sem, d + 2))

        @pl.when(jnp.logical_and(has_down, zz == count - 1))
        def _():
            act(passed(slot, part, line_sem, d - 2))

    def col_copy(slot):
        return pltpu.make_async_remote_copy(
            src_ref=col_parts.at[slot],
            dst_ref=inbox.at[d],
            send_sem=col_send.at[slot],
            recv_sem=col_recv.at[d],
            device_id=(slot, mirror),
            device_id_type=MESH,
        )

    for load in loads:
        load.wait()

    def prepare(slot, carry):
        own = rows[pl.ds(pl.multiple_of(slot * BLOCK, BLOCK), BLOCK), :]
        flipped = own.T
        turned[slot] = flipped
        values = flipped.astype(jnp.float32)
        total = jnp.sum(lane_fold(values * values), axis=0, keepdims=True)
        scale = (SHARPNESS * LOG2_E) / jnp.sqrt(total + EPSILON)
        inv_home[slot] = jnp.broadcast_to(scale, (8, BLOCK))
        home_acc[slot] = jnp.zeros((8, BLOCK), jnp.float32)
        return carry

    later = range(PARTS // 2, PARTS)
    done = 0
    for i, part in enumerate(later):
        upto = slots * (i + 1) // len(later)
        lax.fori_loop(done, upto, prepare, 0)
        done = upto
        own_each(lambda copy: copy.start(), (part,))

    def compute(slot):
        visitor = blocks[slot]
        values = visitor.astype(jnp.float32)
        inv = 1.0 / jnp.sqrt(jnp.sum(values * values, axis=1, keepdims=True) + EPSILON)
        guest_acc = jnp.zeros((BLOCK, 128), jnp.float32)
        for s in range(slots):
            products = jnp.dot(visitor, turned[s], preferred_element_type=jnp.float32)
            tile = jnp.exp2(products * inv * inv_home[s, 0:1, :])
            listed = mask[s, 0, slot].astype(jnp.float32)
            home_acc[s] += lane_fold(tile) * listed
            guest_acc += (tile[:, :128] + tile[:, 128:]) * listed
        col_parts[slot] = lane_fold(guest_acc.T)
        col_copy(slot).start()

    def both_ways(dist, act):
        def way(plus, carry):
            zz = z + (2 * plus - 1) * dist
            valid = (dist >= 0) & (zz >= 0) & (zz < count)
            valid = valid & jnp.logical_not((dist == 0) & (plus == 1))

            @pl.when(valid)
            def _():
                act(zz)

            return carry

        lax.fori_loop(0, 2, way, 0)

    def arrive(zz, xx, part):
        passed(zz * 2 + xx, part, line_sem, d).wait_recv()

    def line_part(part):
        def act(zz):
            arrive(zz, x, part)
            line_each(zz, part, lambda copy: copy.start())

        return act

    def end_parts(zz):
        @pl.when(is_end(zz))
        def _():
            for part in range(PARTS // 2, PARTS):
                arrive(zz, 1 - x, part)
                end_each(zz, part, lambda copy: copy.start())

    def side_compute(zz):
        for part in range(PARTS // 2):
            arrive(zz, 1 - x, part)

        @pl.when(jnp.logical_not(is_end(zz)))
        def _():
            for part in range(PARTS // 2, PARTS):
                arrive(zz, 1 - x, part)

        compute(zz * 2 + 1 - x)

    def step(k, carry):
        for part in range(PARTS // 2):
            both_ways(k, line_part(part))
        both_ways(k - 2, side_compute)
        for part in range(PARTS // 2, PARTS):
            both_ways(k, line_part(part))
        both_ways(k, lambda zz: compute(zz * 2 + x))
        both_ways(k - 1, end_parts)
        return carry

    lax.fori_loop(0, count + 2, step, 0)

    device = d * n_cluster + c
    home_list = home_ids[...]
    guest_list = guest_ids[...]

    def pick(ids, place):
        here = lax.broadcasted_iota(jnp.int32, ids.shape, 1) == place
        return jnp.sum(jnp.where(here, ids, 0), axis=1, keepdims=True)

    def log_members(own_id):
        number = jnp.sum((home_list == own_id).astype(jnp.int32), axis=1, keepdims=True)
        number += jnp.sum((guest_list == own_id).astype(jnp.int32), axis=1, keepdims=True)
        return jnp.log(number.astype(jnp.float32))

    for s in range(slots):
        density = jnp.sum(home_acc[s], axis=0, keepdims=True)
        score = jnp.log(1.0 + density) - log_members(pick(home_list, device * slots + s))
        home_out[:, s * BLOCK : (s + 1) * BLOCK] = score
    log_guest = log_members(pick(guest_list, device))

    own_each(lambda copy: copy.wait_send(), range(PARTS))

    def drain(t, carry):
        for part in range(PARTS):
            line_each(t, part, lambda copy: copy.wait_send())
        for part in range(PARTS // 2, PARTS):
            end_each(t, part, lambda copy: copy.wait_send())
        return carry

    lax.fori_loop(0, count, drain, 0)

    def collect(t, total):
        pltpu.make_async_remote_copy(
            src_ref=col_parts.at[t],
            dst_ref=inbox.at[t],
            send_sem=col_send.at[t],
            recv_sem=col_recv.at[t],
            device_id=(t, mirror),
            device_id_type=MESH,
        ).wait_recv()
        return total + inbox[t]

    total = lax.fori_loop(0, ndp, collect, jnp.zeros((8, BLOCK), jnp.float32))
    guest_out[...] = jnp.log(1.0 + jnp.sum(total, axis=0, keepdims=True)) - log_guest

    def col_drain(t, carry):
        col_copy(t).wait_send()
        return carry

    lax.fori_loop(0, ndp, col_drain, 0)


def body(home_rows, guest_rows, home_cluster, guest_cluster, pair_mask):
    slots = home_rows.shape[0] // BLOCK
    width = home_rows.shape[1]
    ndp = lax.axis_size("dp")
    hbm = pl.BlockSpec(memory_space=pltpu.HBM)
    vmem = pl.BlockSpec(memory_space=pltpu.VMEM)
    pairs = slots * ndp * BLOCK * BLOCK
    home_score, guest_score = pl.pallas_call(
        functools.partial(kernel, ndp, slots),
        out_shape=(
            pltpu.VMEM((1, slots * BLOCK), jnp.float32),
            pltpu.VMEM((1, BLOCK), jnp.float32),
        ),
        in_specs=[hbm] * 5,
        out_specs=(vmem, vmem),
        scratch_shapes=[
            pltpu.VMEM((slots * BLOCK, width), jnp.bfloat16),
            pltpu.VMEM((slots, width, BLOCK), jnp.bfloat16),
            pltpu.VMEM((ndp, BLOCK, width), jnp.bfloat16),
            pltpu.VMEM((slots, 8, BLOCK), jnp.float32),
            pltpu.VMEM((slots, 8, BLOCK), jnp.float32),
            pltpu.VMEM((ndp, 8, BLOCK), jnp.float32),
            pltpu.VMEM((ndp, 8, BLOCK), jnp.float32),
            pltpu.VMEM((1, home_cluster.shape[0]), jnp.int32),
            pltpu.VMEM((1, guest_cluster.shape[0]), jnp.int32),
            pltpu.SMEM((slots, 1, ndp), jnp.int32),
            pltpu.SemaphoreType.DMA((4,)),
            pltpu.SemaphoreType.DMA((4, PARTS)),
            pltpu.SemaphoreType.DMA((ndp, PARTS)),
            pltpu.SemaphoreType.DMA((ndp, PARTS)),
            pltpu.SemaphoreType.DMA((ndp, PARTS)),
            pltpu.SemaphoreType.DMA((ndp,)),
            pltpu.SemaphoreType.DMA((ndp,)),
        ],
        compiler_params=pltpu.CompilerParams(
            collective_id=0, has_side_effects=True, vmem_limit_bytes=62 * 2**20
        ),
        cost_estimate=pl.CostEstimate(
            flops=2 * pairs * width,
            bytes_accessed=2 * (home_rows.size + ndp * BLOCK * width),
            transcendentals=pairs,
        ),
    )(
        home_rows,
        guest_rows,
        home_cluster.reshape(1, -1),
        guest_cluster.reshape(1, -1),
        pair_mask.transpose(1, 0, 2),
    )
    return (home_score.reshape(-1), guest_score.reshape(-1))


def solution(mesh):
    placed = (
        P(("dp", "cluster"), None),
        P(("dp", "cluster"), None),
        P(),
        P(),
        P(("dp", "cluster"), None, None),
    )
    return jax.shard_map(
        body,
        mesh=mesh,
        in_specs=placed,
        out_specs=(P(("dp", "cluster")), P(("dp", "cluster"))),
        check_vma=False,
    )
```

```python
import functools

import jax
import jax.numpy as jnp
from jax import lax
from jax.experimental import pallas as pl
from jax.experimental.pallas import tpu as pltpu
from jax.sharding import PartitionSpec as P

BLOCK = 256
PARTS = 4
CHUNK = BLOCK // PARTS

SHARPNESS = 30.0
EPSILON = 1e-06
MESH = pl.DeviceIdType.MESH


def lane_fold(value):
    return jnp.sum(value.reshape(value.shape[0] // 8, 8, value.shape[1]), axis=0)


def kernel(
    ndp, slots, home_ref, guest_ref, home_hbm, guest_hbm, mask_hbm, home_out, guest_out,
    rows, turned, blocks, inv_home, home_acc, col_parts, inbox, home_ids, guest_ids, mask,
    load_sem, own_sem, line_sem, side_sem, recv_sem, col_send, col_recv,
):
    d = lax.axis_index("dp")
    c = lax.axis_index("cluster")
    n_cluster = lax.axis_size("cluster")
    count = ndp // 2
    z = lax.div(d, 2)
    x = lax.rem(d, 2)
    mirror = c + 1 - 2 * lax.rem(c, 2)
    beside = d + 1 - 2 * x
    has_up = z < count - 1
    has_down = z > 0

    barrier = pltpu.get_barrier_semaphore()

    def greet(dp, cluster):
        pl.semaphore_signal(barrier, inc=1, device_id=(dp, cluster), device_id_type=MESH)

    greet(d, mirror)
    for column in (c, mirror):
        greet(beside, column)

        @pl.when(has_up)
        def _():
            greet(d + 2, column)

        @pl.when(has_down)
        def _():
            greet(d - 2, column)

    loads = [
        pltpu.make_async_copy(source, target, load_sem.at[i])
        for i, (source, target) in enumerate(
            ((home_ref, rows), (home_hbm, home_ids), (guest_hbm, guest_ids), (mask_hbm, mask))
        )
    ]
    for load in loads:
        load.start()

    pl.semaphore_wait(barrier, 3 + 2 * has_up.astype(jnp.int32) + 2 * has_down.astype(jnp.int32))

    def piece(part):
        return pl.ds(part * CHUNK, CHUNK)

    def own_copy(part, way, target):
        return pltpu.make_async_remote_copy(
            src_ref=guest_ref.at[piece(part), :],
            dst_ref=blocks.at[d, piece(part), :],
            send_sem=own_sem.at[way, part],
            recv_sem=recv_sem.at[d, part],
            device_id=(target, mirror),
            device_id_type=MESH,
        )

    def own_each(act, parts):
        for part in parts:

            @pl.when(has_up)
            def _():
                act(own_copy(part, 0, d + 2))

            @pl.when(has_down)
            def _():
                act(own_copy(part, 1, d - 2))

            act(own_copy(part, 2, beside))
            act(own_copy(part, 3, d))

    own_each(lambda copy: copy.start(), range(PARTS // 2))

    def passed(slot, part, sem, target):
        return pltpu.make_async_remote_copy(
            src_ref=blocks.at[slot, piece(part), :],
            dst_ref=blocks.at[slot, piece(part), :],
            send_sem=sem.at[slot, part],
            recv_sem=recv_sem.at[slot, part],
            device_id=(target, c),
            device_id_type=MESH,
        )

    def is_end(zz):
        return jnp.logical_or(zz == 0, zz == count - 1)

    def line_each(zz, part, act):
        slot = zz * 2 + x

        @pl.when(jnp.logical_and(has_up, zz < z))
        def _():
            act(passed(slot, part, line_sem, d + 2))

        @pl.when(jnp.logical_and(has_down, zz > z))
        def _():
            act(passed(slot, part, line_sem, d - 2))

        by_side = zz != z
        if part >= PARTS // 2:
            by_side = jnp.logical_and(by_side, jnp.logical_not(is_end(zz)))

        @pl.when(by_side)
        def _():
            act(passed(slot, part, side_sem, beside))

    def end_each(zz, part, act):
        slot = zz * 2 + 1 - x

        @pl.when(jnp.logical_and(has_up, zz == 0))
        def _():
            act(passed(slot, part, line_sem, d + 2))

        @pl.when(jnp.logical_and(has_down, zz == count - 1))
        def _():
            act(passed(slot, part, line_sem, d - 2))

    def col_copy(slot):
        return pltpu.make_async_remote_copy(
            src_ref=col_parts.at[slot],
            dst_ref=inbox.at[d],
            send_sem=col_send.at[slot],
            recv_sem=col_recv.at[d],
            device_id=(slot, mirror),
            device_id_type=MESH,
        )

    for load in loads:
        load.wait()

    def prepare(slot, carry):
        own = rows[pl.ds(pl.multiple_of(slot * BLOCK, BLOCK), BLOCK), :]
        flipped = own.T
        turned[slot] = flipped
        values = flipped.astype(jnp.float32)
        total = jnp.sum(lane_fold(values * values), axis=0, keepdims=True)
        scale = SHARPNESS / jnp.sqrt(total + EPSILON)
        inv_home[slot] = jnp.broadcast_to(scale, (8, BLOCK))
        home_acc[slot] = jnp.zeros((8, BLOCK), jnp.float32)
        return carry

    later = range(PARTS // 2, PARTS)
    done = 0
    for i, part in enumerate(later):
        upto = slots * (i + 1) // len(later)
        lax.fori_loop(done, upto, prepare, 0)
        done = upto
        own_each(lambda copy: copy.start(), (part,))

    def compute(slot, first, extent):
        visitor = blocks[slot, first : first + extent, :]
        values = visitor.astype(jnp.float32)
        inv = 1.0 / jnp.sqrt(jnp.sum(values * values, axis=1, keepdims=True) + EPSILON)
        inv = jnp.broadcast_to(inv, (extent, 128))
        guest_acc = jnp.zeros((extent, 128), jnp.float32)
        for s in range(slots):
            products = jnp.dot(visitor, turned[s], preferred_element_type=jnp.float32)
            listed = mask[s, 0, slot].astype(jnp.float32)
            both = jnp.zeros((extent, 128), jnp.float32)
            for lanes in (slice(0, 128), slice(128, 256)):
                tile = jnp.exp(products[:, lanes] * inv * inv_home[s, 0:1, lanes])
                home_acc[s, :, lanes] += lane_fold(tile) * listed
                both += tile
            guest_acc += both * listed
        col_parts[slot, :, first : first + extent] = lane_fold(guest_acc.T)

    def compute_all(slot):
        compute(slot, 0, BLOCK)
        col_copy(slot).start()

    def both_ways(dist, act):
        def way(plus, carry):
            zz = z + (2 * plus - 1) * dist
            valid = (dist >= 0) & (zz >= 0) & (zz < count)
            valid = valid & jnp.logical_not((dist == 0) & (plus == 1))

            @pl.when(valid)
            def _():
                act(zz)

            return carry

        lax.fori_loop(0, 2, way, 0)

    def arrive(zz, xx, part):
        passed(zz * 2 + xx, part, line_sem, d).wait_recv()

    def line_part(part):
        def act(zz):
            arrive(zz, x, part)
            line_each(zz, part, lambda copy: copy.start())

        return act

    def end_parts(zz):
        @pl.when(is_end(zz))
        def _():
            for part in range(PARTS // 2, PARTS):
                arrive(zz, 1 - x, part)
                end_each(zz, part, lambda copy: copy.start())

    def side_compute(zz):
        for part in range(PARTS // 2):
            arrive(zz, 1 - x, part)

        @pl.when(jnp.logical_not(is_end(zz)))
        def _():
            for part in range(PARTS // 2, PARTS):
                arrive(zz, 1 - x, part)

        compute_all(zz * 2 + 1 - x)

    def step(k, carry):
        for part in range(PARTS // 2):
            both_ways(k, line_part(part))
        both_ways(k - 2, side_compute)
        for part in range(PARTS // 2, PARTS):
            both_ways(k, line_part(part))
        both_ways(k, lambda zz: compute_all(zz * 2 + x))
        both_ways(k - 1, end_parts)
        return carry

    lax.fori_loop(0, count, step, 0)
    both_ways(count - 2, side_compute)

    def far_compute(zz):
        slot = zz * 2 + 1 - x
        for half in range(2):
            for part in range(half * PARTS // 2, (half + 1) * PARTS // 2):
                arrive(zz, 1 - x, part)
            compute(slot, half * BLOCK // 2, BLOCK // 2)
        col_copy(slot).start()

    both_ways(count - 1, far_compute)

    device = d * n_cluster + c
    home_list = home_ids[...]
    guest_list = guest_ids[...]

    def pick(ids, place):
        here = lax.broadcasted_iota(jnp.int32, ids.shape, 1) == place
        return jnp.sum(jnp.where(here, ids, 0), axis=1, keepdims=True)

    def log_members(own_id):
        number = jnp.sum((home_list == own_id).astype(jnp.int32), axis=1, keepdims=True)
        number += jnp.sum((guest_list == own_id).astype(jnp.int32), axis=1, keepdims=True)
        return jnp.log(number.astype(jnp.float32))

    for s in range(slots):
        density = jnp.sum(home_acc[s], axis=0, keepdims=True)
        score = jnp.log(1.0 + density) - log_members(pick(home_list, device * slots + s))
        home_out[:, s * BLOCK : (s + 1) * BLOCK] = score
    log_guest = log_members(pick(guest_list, device))

    own_each(lambda copy: copy.wait_send(), range(PARTS))

    def drain(t, carry):
        for part in range(PARTS):
            line_each(t, part, lambda copy: copy.wait_send())
        for part in range(PARTS // 2, PARTS):
            end_each(t, part, lambda copy: copy.wait_send())
        return carry

    lax.fori_loop(0, count, drain, 0)

    def collect(t, total):
        pltpu.make_async_remote_copy(
            src_ref=col_parts.at[t],
            dst_ref=inbox.at[t],
            send_sem=col_send.at[t],
            recv_sem=col_recv.at[t],
            device_id=(t, mirror),
            device_id_type=MESH,
        ).wait_recv()
        return total + inbox[t]

    total = lax.fori_loop(0, ndp, collect, jnp.zeros((8, BLOCK), jnp.float32))
    guest_out[...] = jnp.log(1.0 + jnp.sum(total, axis=0, keepdims=True)) - log_guest

    def col_drain(t, carry):
        col_copy(t).wait_send()
        return carry

    lax.fori_loop(0, ndp, col_drain, 0)


def body(home_rows, guest_rows, home_cluster, guest_cluster, pair_mask):
    slots = home_rows.shape[0] // BLOCK
    width = home_rows.shape[1]
    ndp = lax.axis_size("dp")
    hbm = pl.BlockSpec(memory_space=pltpu.HBM)
    vmem = pl.BlockSpec(memory_space=pltpu.VMEM)
    pairs = slots * ndp * BLOCK * BLOCK
    home_score, guest_score = pl.pallas_call(
        functools.partial(kernel, ndp, slots),
        out_shape=(
            pltpu.VMEM((1, slots * BLOCK), jnp.float32),
            pltpu.VMEM((1, BLOCK), jnp.float32),
        ),
        in_specs=[hbm] * 5,
        out_specs=(vmem, vmem),
        scratch_shapes=[
            pltpu.VMEM((slots * BLOCK, width), jnp.bfloat16),
            pltpu.VMEM((slots, width, BLOCK), jnp.bfloat16),
            pltpu.VMEM((ndp, BLOCK, width), jnp.bfloat16),
            pltpu.VMEM((slots, 8, BLOCK), jnp.float32),
            pltpu.VMEM((slots, 8, BLOCK), jnp.float32),
            pltpu.VMEM((ndp, 8, BLOCK), jnp.float32),
            pltpu.VMEM((ndp, 8, BLOCK), jnp.float32),
            pltpu.VMEM((1, home_cluster.shape[0]), jnp.int32),
            pltpu.VMEM((1, guest_cluster.shape[0]), jnp.int32),
            pltpu.SMEM((slots, 1, ndp), jnp.int32),
            pltpu.SemaphoreType.DMA((4,)),
            pltpu.SemaphoreType.DMA((4, PARTS)),
            pltpu.SemaphoreType.DMA((ndp, PARTS)),
            pltpu.SemaphoreType.DMA((ndp, PARTS)),
            pltpu.SemaphoreType.DMA((ndp, PARTS)),
            pltpu.SemaphoreType.DMA((ndp,)),
            pltpu.SemaphoreType.DMA((ndp,)),
        ],
        compiler_params=pltpu.CompilerParams(
            collective_id=0, has_side_effects=True, vmem_limit_bytes=62 * 2**20
        ),
        cost_estimate=pl.CostEstimate(
            flops=2 * pairs * width,
            bytes_accessed=2 * (home_rows.size + ndp * BLOCK * width),
            transcendentals=pairs,
        ),
    )(
        home_rows,
        guest_rows,
        home_cluster.reshape(1, -1),
        guest_cluster.reshape(1, -1),
        pair_mask.transpose(1, 0, 2),
    )
    return (home_score.reshape(-1), guest_score.reshape(-1))


def solution(mesh):
    placed = (
        P(("dp", "cluster"), None),
        P(("dp", "cluster"), None),
        P(),
        P(),
        P(("dp", "cluster"), None, None),
    )
    return jax.shard_map(
        body,
        mesh=mesh,
        in_specs=placed,
        out_specs=(P(("dp", "cluster")), P(("dp", "cluster"))),
        check_vma=False,
    )
```

```python
import functools

import jax
import jax.numpy as jnp
from jax import lax
from jax.experimental import pallas as pl
from jax.experimental.pallas import tpu as pltpu
from jax.sharding import PartitionSpec as P

BLOCK = 256
PARTS = 4
CHUNK = BLOCK // PARTS

SHARPNESS = 30.0
EPSILON = 1e-06
MESH = pl.DeviceIdType.MESH


def lane_fold(value):
    return jnp.sum(value.reshape(value.shape[0] // 8, 8, value.shape[1]), axis=0)


def kernel(
    ndp, slots, home_ref, guest_ref, home_hbm, guest_hbm, mask_hbm, home_out, guest_out,
    rows, turned, blocks, inv_home, home_acc, col_parts, inbox, home_ids, guest_ids, mask,
    load_sem, own_sem, line_sem, side_sem, recv_sem, col_send, col_recv,
):
    d = lax.axis_index("dp")
    c = lax.axis_index("cluster")
    n_cluster = lax.axis_size("cluster")
    count = ndp // 2
    z = lax.div(d, 2)
    x = lax.rem(d, 2)
    mirror = c + 1 - 2 * lax.rem(c, 2)
    beside = d + 1 - 2 * x
    has_up = z < count - 1
    has_down = z > 0

    barrier = pltpu.get_barrier_semaphore()

    def greet(dp, cluster):
        pl.semaphore_signal(barrier, inc=1, device_id=(dp, cluster), device_id_type=MESH)

    greet(d, mirror)
    for column in (c, mirror):
        greet(beside, column)

        @pl.when(has_up)
        def _():
            greet(d + 2, column)

        @pl.when(has_down)
        def _():
            greet(d - 2, column)

    loads = [
        pltpu.make_async_copy(source, target, load_sem.at[i])
        for i, (source, target) in enumerate(
            ((home_ref, rows), (home_hbm, home_ids), (guest_hbm, guest_ids), (mask_hbm, mask))
        )
    ]
    for load in loads:
        load.start()

    pl.semaphore_wait(barrier, 3 + 2 * has_up.astype(jnp.int32) + 2 * has_down.astype(jnp.int32))

    def piece(part):
        return pl.ds(part * CHUNK, CHUNK)

    def own_copy(part, way, target):
        return pltpu.make_async_remote_copy(
            src_ref=guest_ref.at[piece(part), :],
            dst_ref=blocks.at[d, piece(part), :],
            send_sem=own_sem.at[way, part],
            recv_sem=recv_sem.at[d, part],
            device_id=(target, mirror),
            device_id_type=MESH,
        )

    def own_each(act, parts):
        for part in parts:

            @pl.when(has_up)
            def _():
                act(own_copy(part, 0, d + 2))

            @pl.when(has_down)
            def _():
                act(own_copy(part, 1, d - 2))

            act(own_copy(part, 2, beside))
            act(own_copy(part, 3, d))

    own_each(lambda copy: copy.start(), range(PARTS // 2))

    def passed(slot, part, sem, target):
        return pltpu.make_async_remote_copy(
            src_ref=blocks.at[slot, piece(part), :],
            dst_ref=blocks.at[slot, piece(part), :],
            send_sem=sem.at[slot, part],
            recv_sem=recv_sem.at[slot, part],
            device_id=(target, c),
            device_id_type=MESH,
        )

    def is_end(zz):
        return jnp.logical_or(zz == 0, zz == count - 1)

    def line_each(zz, part, act):
        slot = zz * 2 + x

        @pl.when(jnp.logical_and(has_up, zz < z))
        def _():
            act(passed(slot, part, line_sem, d + 2))

        @pl.when(jnp.logical_and(has_down, zz > z))
        def _():
            act(passed(slot, part, line_sem, d - 2))

        by_side = zz != z
        if part >= PARTS // 2:
            by_side = jnp.logical_and(by_side, jnp.logical_not(is_end(zz)))

        @pl.when(by_side)
        def _():
            act(passed(slot, part, side_sem, beside))

    def end_each(zz, part, act):
        slot = zz * 2 + 1 - x

        @pl.when(jnp.logical_and(has_up, zz == 0))
        def _():
            act(passed(slot, part, line_sem, d + 2))

        @pl.when(jnp.logical_and(has_down, zz == count - 1))
        def _():
            act(passed(slot, part, line_sem, d - 2))

    def col_copy(slot):
        return pltpu.make_async_remote_copy(
            src_ref=col_parts.at[slot],
            dst_ref=inbox.at[d],
            send_sem=col_send.at[slot],
            recv_sem=col_recv.at[d],
            device_id=(slot, mirror),
            device_id_type=MESH,
        )

    for load in loads:
        load.wait()

    def prepare(slot, carry):
        own = rows[pl.ds(pl.multiple_of(slot * BLOCK, BLOCK), BLOCK), :]
        flipped = own.T
        turned[slot] = flipped
        values = flipped.astype(jnp.float32)
        total = jnp.sum(lane_fold(values * values), axis=0, keepdims=True)
        scale = SHARPNESS / jnp.sqrt(total + EPSILON)
        inv_home[slot] = jnp.broadcast_to(scale, (8, BLOCK))
        home_acc[slot] = jnp.zeros((8, BLOCK), jnp.float32)
        return carry

    later = range(PARTS // 2, PARTS)
    done = 0
    for i, part in enumerate(later):
        upto = slots * (i + 1) // len(later)
        lax.fori_loop(done, upto, prepare, 0)
        done = upto
        own_each(lambda copy: copy.start(), (part,))

    def compute(slot, first, extent):
        visitor = blocks[slot, first : first + extent, :]
        values = visitor.astype(jnp.float32)
        inv = 1.0 / jnp.sqrt(jnp.sum(values * values, axis=1, keepdims=True) + EPSILON)
        inv = jnp.broadcast_to(inv, (extent, 128))
        guest_acc = jnp.zeros((extent, 128), jnp.float32)
        for s in range(slots):
            products = jnp.dot(visitor, turned[s], preferred_element_type=jnp.float32)
            listed = mask[s, 0, slot].astype(jnp.float32)
            both = jnp.zeros((extent, 128), jnp.float32)
            for lanes in (slice(0, 128), slice(128, 256)):
                tile = jnp.exp(products[:, lanes] * inv * inv_home[s, 0:1, lanes])
                home_acc[s, :, lanes] += lane_fold(tile) * listed
                both += tile
            guest_acc += both * listed
        col_parts[slot, :, first : first + extent] = lane_fold(guest_acc.T)

    def compute_all(slot):
        compute(slot, 0, BLOCK)
        col_copy(slot).start()

    def both_ways(dist, act):
        def way(plus, carry):
            zz = z + (2 * plus - 1) * dist
            valid = (dist >= 0) & (zz >= 0) & (zz < count)
            valid = valid & jnp.logical_not((dist == 0) & (plus == 1))

            @pl.when(valid)
            def _():
                act(zz)

            return carry

        lax.fori_loop(0, 2, way, 0)

    def arrive(zz, xx, part):
        passed(zz * 2 + xx, part, line_sem, d).wait_recv()

    def line_part(part):
        def act(zz):
            arrive(zz, x, part)
            line_each(zz, part, lambda copy: copy.start())

        return act

    def end_parts(zz):
        @pl.when(is_end(zz))
        def _():
            for part in range(PARTS // 2, PARTS):
                arrive(zz, 1 - x, part)
                end_each(zz, part, lambda copy: copy.start())

    def side_compute(zz):
        for part in range(PARTS // 2):
            arrive(zz, 1 - x, part)

        @pl.when(jnp.logical_not(is_end(zz)))
        def _():
            for part in range(PARTS // 2, PARTS):
                arrive(zz, 1 - x, part)

        compute_all(zz * 2 + 1 - x)

    def step(k, carry):
        both_ways(jnp.where(k > 1, k - 1, -1), end_parts)
        both_ways(k - 2, side_compute)
        for part in range(PARTS):
            both_ways(k, line_part(part))
        both_ways(jnp.where(k == 1, 0, -1), end_parts)
        both_ways(k, lambda zz: compute_all(zz * 2 + x))
        return carry

    lax.fori_loop(0, count, step, 0)
    both_ways(count - 2, side_compute)

    def far_compute(zz):
        slot = zz * 2 + 1 - x
        for half in range(2):
            for part in range(half * PARTS // 2, (half + 1) * PARTS // 2):
                arrive(zz, 1 - x, part)
            compute(slot, half * BLOCK // 2, BLOCK // 2)
        col_copy(slot).start()

    both_ways(count - 1, far_compute)

    device = d * n_cluster + c
    home_list = home_ids[...]
    guest_list = guest_ids[...]

    def pick(ids, place):
        here = lax.broadcasted_iota(jnp.int32, ids.shape, 1) == place
        return jnp.sum(jnp.where(here, ids, 0), axis=1, keepdims=True)

    def log_members(own_id):
        number = jnp.sum((home_list == own_id).astype(jnp.int32), axis=1, keepdims=True)
        number += jnp.sum((guest_list == own_id).astype(jnp.int32), axis=1, keepdims=True)
        return jnp.log(number.astype(jnp.float32))

    for s in range(slots):
        density = jnp.sum(home_acc[s], axis=0, keepdims=True)
        score = jnp.log(1.0 + density) - log_members(pick(home_list, device * slots + s))
        home_out[:, s * BLOCK : (s + 1) * BLOCK] = score
    log_guest = log_members(pick(guest_list, device))

    own_each(lambda copy: copy.wait_send(), range(PARTS))

    def drain(t, carry):
        for part in range(PARTS):
            line_each(t, part, lambda copy: copy.wait_send())
        for part in range(PARTS // 2, PARTS):
            end_each(t, part, lambda copy: copy.wait_send())
        return carry

    lax.fori_loop(0, count, drain, 0)

    def collect(t, total):
        pltpu.make_async_remote_copy(
            src_ref=col_parts.at[t],
            dst_ref=inbox.at[t],
            send_sem=col_send.at[t],
            recv_sem=col_recv.at[t],
            device_id=(t, mirror),
            device_id_type=MESH,
        ).wait_recv()
        return total + inbox[t]

    total = lax.fori_loop(0, ndp, collect, jnp.zeros((8, BLOCK), jnp.float32))
    guest_out[...] = jnp.log(1.0 + jnp.sum(total, axis=0, keepdims=True)) - log_guest

    def col_drain(t, carry):
        col_copy(t).wait_send()
        return carry

    lax.fori_loop(0, ndp, col_drain, 0)


def body(home_rows, guest_rows, home_cluster, guest_cluster, pair_mask):
    slots = home_rows.shape[0] // BLOCK
    width = home_rows.shape[1]
    ndp = lax.axis_size("dp")
    hbm = pl.BlockSpec(memory_space=pltpu.HBM)
    vmem = pl.BlockSpec(memory_space=pltpu.VMEM)
    pairs = slots * ndp * BLOCK * BLOCK
    home_score, guest_score = pl.pallas_call(
        functools.partial(kernel, ndp, slots),
        out_shape=(
            pltpu.VMEM((1, slots * BLOCK), jnp.float32),
            pltpu.VMEM((1, BLOCK), jnp.float32),
        ),
        in_specs=[hbm] * 5,
        out_specs=(vmem, vmem),
        scratch_shapes=[
            pltpu.VMEM((slots * BLOCK, width), jnp.bfloat16),
            pltpu.VMEM((slots, width, BLOCK), jnp.bfloat16),
            pltpu.VMEM((ndp, BLOCK, width), jnp.bfloat16),
            pltpu.VMEM((slots, 8, BLOCK), jnp.float32),
            pltpu.VMEM((slots, 8, BLOCK), jnp.float32),
            pltpu.VMEM((ndp, 8, BLOCK), jnp.float32),
            pltpu.VMEM((ndp, 8, BLOCK), jnp.float32),
            pltpu.VMEM((1, home_cluster.shape[0]), jnp.int32),
            pltpu.VMEM((1, guest_cluster.shape[0]), jnp.int32),
            pltpu.SMEM((slots, 1, ndp), jnp.int32),
            pltpu.SemaphoreType.DMA((4,)),
            pltpu.SemaphoreType.DMA((4, PARTS)),
            pltpu.SemaphoreType.DMA((ndp, PARTS)),
            pltpu.SemaphoreType.DMA((ndp, PARTS)),
            pltpu.SemaphoreType.DMA((ndp, PARTS)),
            pltpu.SemaphoreType.DMA((ndp,)),
            pltpu.SemaphoreType.DMA((ndp,)),
        ],
        compiler_params=pltpu.CompilerParams(
            collective_id=0, has_side_effects=True, vmem_limit_bytes=62 * 2**20
        ),
        cost_estimate=pl.CostEstimate(
            flops=2 * pairs * width,
            bytes_accessed=2 * (home_rows.size + ndp * BLOCK * width),
            transcendentals=pairs,
        ),
    )(
        home_rows,
        guest_rows,
        home_cluster.reshape(1, -1),
        guest_cluster.reshape(1, -1),
        pair_mask.transpose(1, 0, 2),
    )
    return (home_score.reshape(-1), guest_score.reshape(-1))


def solution(mesh):
    placed = (
        P(("dp", "cluster"), None),
        P(("dp", "cluster"), None),
        P(),
        P(),
        P(("dp", "cluster"), None, None),
    )
    return jax.shard_map(
        body,
        mesh=mesh,
        in_specs=placed,
        out_specs=(P(("dp", "cluster")), P(("dp", "cluster"))),
        check_vma=False,
    )
```

```python
import functools

import jax
import jax.numpy as jnp
from jax import lax
from jax.experimental import pallas as pl
from jax.experimental.pallas import tpu as pltpu
from jax.sharding import PartitionSpec as P

BLOCK = 256
PARTS = 4
CHUNK = BLOCK // PARTS
BY_SIDE = PARTS

SHARPNESS = 30.0
EPSILON = 1e-06
MESH = pl.DeviceIdType.MESH


def lane_fold(value):
    return jnp.sum(value.reshape(value.shape[0] // 8, 8, value.shape[1]), axis=0)


def kernel(
    ndp, slots, home_ref, guest_ref, home_hbm, guest_hbm, mask_hbm, home_out, guest_out,
    rows, turned, blocks, inv_home, home_acc, col_parts, inbox, home_ids, guest_ids, mask,
    load_sem, own_sem, line_sem, side_sem, recv_sem, col_send, col_recv,
):
    d = lax.axis_index("dp")
    c = lax.axis_index("cluster")
    n_cluster = lax.axis_size("cluster")
    count = ndp // 2
    z = lax.div(d, 2)
    x = lax.rem(d, 2)
    mirror = c + 1 - 2 * lax.rem(c, 2)
    beside = d + 1 - 2 * x
    has_up = z < count - 1
    has_down = z > 0

    barrier = pltpu.get_barrier_semaphore()

    def greet(dp, cluster):
        pl.semaphore_signal(barrier, inc=1, device_id=(dp, cluster), device_id_type=MESH)

    greet(d, mirror)
    for column in (c, mirror):
        greet(beside, column)

        @pl.when(has_up)
        def _():
            greet(d + 2, column)

        @pl.when(has_down)
        def _():
            greet(d - 2, column)

    loads = [
        pltpu.make_async_copy(source, target, load_sem.at[i])
        for i, (source, target) in enumerate(
            ((home_ref, rows), (home_hbm, home_ids), (guest_hbm, guest_ids), (mask_hbm, mask))
        )
    ]
    for load in loads:
        load.start()

    pl.semaphore_wait(barrier, 3 + 2 * has_up.astype(jnp.int32) + 2 * has_down.astype(jnp.int32))

    def piece(part):
        return pl.ds(part * CHUNK, CHUNK)

    def own_copy(part, way, target):
        return pltpu.make_async_remote_copy(
            src_ref=guest_ref.at[piece(part), :],
            dst_ref=blocks.at[d, piece(part), :],
            send_sem=own_sem.at[way, part],
            recv_sem=recv_sem.at[d, part],
            device_id=(target, mirror),
            device_id_type=MESH,
        )

    def own_each(act, parts):
        for part in parts:

            @pl.when(has_up)
            def _():
                act(own_copy(part, 0, d + 2))

            @pl.when(has_down)
            def _():
                act(own_copy(part, 1, d - 2))

            act(own_copy(part, 2, beside))
            act(own_copy(part, 3, d))

    own_each(lambda copy: copy.start(), range(PARTS // 2))

    def passed(slot, part, sem, target):
        return pltpu.make_async_remote_copy(
            src_ref=blocks.at[slot, piece(part), :],
            dst_ref=blocks.at[slot, piece(part), :],
            send_sem=sem.at[slot, part],
            recv_sem=recv_sem.at[slot, part],
            device_id=(target, c),
            device_id_type=MESH,
        )

    def is_end(zz):
        return jnp.logical_or(zz == 0, zz == count - 1)

    def line_each(zz, part, act):
        slot = zz * 2 + x

        @pl.when(jnp.logical_and(has_up, zz < z))
        def _():
            act(passed(slot, part, line_sem, d + 2))

        @pl.when(jnp.logical_and(has_down, zz > z))
        def _():
            act(passed(slot, part, line_sem, d - 2))

        by_side = zz != z
        if part >= BY_SIDE:
            by_side = jnp.logical_and(by_side, jnp.logical_not(is_end(zz)))

        @pl.when(by_side)
        def _():
            act(passed(slot, part, side_sem, beside))

    def end_each(zz, part, act):
        slot = zz * 2 + 1 - x

        @pl.when(jnp.logical_and(has_up, zz == 0))
        def _():
            act(passed(slot, part, line_sem, d + 2))

        @pl.when(jnp.logical_and(has_down, zz == count - 1))
        def _():
            act(passed(slot, part, line_sem, d - 2))

    def col_copy(slot):
        return pltpu.make_async_remote_copy(
            src_ref=col_parts.at[slot],
            dst_ref=inbox.at[d],
            send_sem=col_send.at[slot],
            recv_sem=col_recv.at[d],
            device_id=(slot, mirror),
            device_id_type=MESH,
        )

    for load in loads:
        load.wait()

    def prepare(slot, carry):
        own = rows[pl.ds(pl.multiple_of(slot * BLOCK, BLOCK), BLOCK), :]
        flipped = own.T
        turned[slot] = flipped
        values = flipped.astype(jnp.float32)
        total = jnp.sum(lane_fold(values * values), axis=0, keepdims=True)
        scale = SHARPNESS * lax.rsqrt(total + EPSILON)
        inv_home[slot] = jnp.broadcast_to(scale, (8, BLOCK))
        home_acc[slot] = jnp.zeros((8, BLOCK), jnp.float32)
        return carry

    later = range(PARTS // 2, PARTS)
    done = 0
    for i, part in enumerate(later):
        upto = slots * (i + 1) // len(later)
        lax.fori_loop(done, upto, prepare, 0)
        done = upto
        own_each(lambda copy: copy.start(), (part,))

    def compute(slot, first, extent):
        visitor = blocks[slot, first : first + extent, :]
        values = visitor.astype(jnp.float32)
        inv = lax.rsqrt(jnp.sum(values * values, axis=1, keepdims=True) + EPSILON)
        inv = jnp.broadcast_to(inv, (extent, 128))
        guest_acc = jnp.zeros((extent, 128), jnp.float32)
        for s in range(slots):
            products = jnp.dot(visitor, turned[s], preferred_element_type=jnp.float32)
            listed = mask[s, 0, slot].astype(jnp.float32)
            both = jnp.zeros((extent, 128), jnp.float32)
            for lanes in (slice(0, 128), slice(128, 256)):
                tile = jnp.exp(products[:, lanes] * inv * inv_home[s, 0:1, lanes])
                home_acc[s, :, lanes] += lane_fold(tile) * listed
                both += tile
            guest_acc += both * listed
        col_parts[slot, :, first : first + extent] = lane_fold(guest_acc.T)

    def compute_all(slot):
        compute(slot, 0, BLOCK)
        col_copy(slot).start()

    def both_ways(dist, act):
        def way(plus, carry):
            zz = z + (2 * plus - 1) * dist
            valid = (dist >= 0) & (zz >= 0) & (zz < count)
            valid = valid & jnp.logical_not((dist == 0) & (plus == 1))

            @pl.when(valid)
            def _():
                act(zz)

            return carry

        lax.fori_loop(0, 2, way, 0)

    def arrive(zz, xx, part):
        passed(zz * 2 + xx, part, line_sem, d).wait_recv()

    def line_part(part):
        def act(zz):
            arrive(zz, x, part)
            line_each(zz, part, lambda copy: copy.start())

        return act

    def end_parts(zz):
        @pl.when(is_end(zz))
        def _():
            for part in range(BY_SIDE, PARTS):
                arrive(zz, 1 - x, part)
                end_each(zz, part, lambda copy: copy.start())

    def side_compute(zz):
        for part in range(BY_SIDE):
            arrive(zz, 1 - x, part)

        @pl.when(jnp.logical_not(is_end(zz)))
        def _():
            for part in range(BY_SIDE, PARTS):
                arrive(zz, 1 - x, part)

        compute_all(zz * 2 + 1 - x)

    def step(k, carry):
        for part in range(PARTS // 2):
            both_ways(k, line_part(part))
        both_ways(k - 2, side_compute)
        for part in range(PARTS // 2, PARTS):
            both_ways(k, line_part(part))
        both_ways(k, lambda zz: compute_all(zz * 2 + x))
        both_ways(k - 1, end_parts)
        return carry

    lax.fori_loop(0, count, step, 0)
    both_ways(count - 2, side_compute)

    def far_compute(zz):
        slot = zz * 2 + 1 - x
        for half in range(2):
            for part in range(half * PARTS // 2, (half + 1) * PARTS // 2):
                arrive(zz, 1 - x, part)
            compute(slot, half * BLOCK // 2, BLOCK // 2)
        col_copy(slot).start()

    both_ways(count - 1, far_compute)

    device = d * n_cluster + c
    home_list = home_ids[...]
    guest_list = guest_ids[...]

    def pick(ids, place):
        here = lax.broadcasted_iota(jnp.int32, ids.shape, 1) == place
        return jnp.sum(jnp.where(here, ids, 0), axis=1, keepdims=True)

    def log_members(own_id):
        number = jnp.sum((home_list == own_id).astype(jnp.int32), axis=1, keepdims=True)
        number += jnp.sum((guest_list == own_id).astype(jnp.int32), axis=1, keepdims=True)
        return jnp.log(number.astype(jnp.float32))

    for s in range(slots):
        density = jnp.sum(home_acc[s], axis=0, keepdims=True)
        score = jnp.log(1.0 + density) - log_members(pick(home_list, device * slots + s))
        home_out[:, s * BLOCK : (s + 1) * BLOCK] = score
    log_guest = log_members(pick(guest_list, device))

    own_each(lambda copy: copy.wait_send(), range(PARTS))

    def drain(t, carry):
        for part in range(PARTS):
            line_each(t, part, lambda copy: copy.wait_send())
        for part in range(BY_SIDE, PARTS):
            end_each(t, part, lambda copy: copy.wait_send())
        return carry

    lax.fori_loop(0, count, drain, 0)

    def collect(t, total):
        pltpu.make_async_remote_copy(
            src_ref=col_parts.at[t],
            dst_ref=inbox.at[t],
            send_sem=col_send.at[t],
            recv_sem=col_recv.at[t],
            device_id=(t, mirror),
            device_id_type=MESH,
        ).wait_recv()
        return total + inbox[t]

    total = lax.fori_loop(0, ndp, collect, jnp.zeros((8, BLOCK), jnp.float32))
    guest_out[...] = jnp.log(1.0 + jnp.sum(total, axis=0, keepdims=True)) - log_guest

    def col_drain(t, carry):
        col_copy(t).wait_send()
        return carry

    lax.fori_loop(0, ndp, col_drain, 0)


def body(home_rows, guest_rows, home_cluster, guest_cluster, pair_mask):
    slots = home_rows.shape[0] // BLOCK
    width = home_rows.shape[1]
    ndp = lax.axis_size("dp")
    hbm = pl.BlockSpec(memory_space=pltpu.HBM)
    vmem = pl.BlockSpec(memory_space=pltpu.VMEM)
    pairs = slots * ndp * BLOCK * BLOCK
    home_score, guest_score = pl.pallas_call(
        functools.partial(kernel, ndp, slots),
        out_shape=(
            pltpu.VMEM((1, slots * BLOCK), jnp.float32),
            pltpu.VMEM((1, BLOCK), jnp.float32),
        ),
        in_specs=[hbm] * 5,
        out_specs=(vmem, vmem),
        scratch_shapes=[
            pltpu.VMEM((slots * BLOCK, width), jnp.bfloat16),
            pltpu.VMEM((slots, width, BLOCK), jnp.bfloat16),
            pltpu.VMEM((ndp, BLOCK, width), jnp.bfloat16),
            pltpu.VMEM((slots, 8, BLOCK), jnp.float32),
            pltpu.VMEM((slots, 8, BLOCK), jnp.float32),
            pltpu.VMEM((ndp, 8, BLOCK), jnp.float32),
            pltpu.VMEM((ndp, 8, BLOCK), jnp.float32),
            pltpu.VMEM((1, home_cluster.shape[0]), jnp.int32),
            pltpu.VMEM((1, guest_cluster.shape[0]), jnp.int32),
            pltpu.SMEM((slots, 1, ndp), jnp.int32),
            pltpu.SemaphoreType.DMA((4,)),
            pltpu.SemaphoreType.DMA((4, PARTS)),
            pltpu.SemaphoreType.DMA((ndp, PARTS)),
            pltpu.SemaphoreType.DMA((ndp, PARTS)),
            pltpu.SemaphoreType.DMA((ndp, PARTS)),
            pltpu.SemaphoreType.DMA((ndp,)),
            pltpu.SemaphoreType.DMA((ndp,)),
        ],
        compiler_params=pltpu.CompilerParams(
            collective_id=0, has_side_effects=True, vmem_limit_bytes=62 * 2**20
        ),
        cost_estimate=pl.CostEstimate(
            flops=2 * pairs * width,
            bytes_accessed=2 * (home_rows.size + ndp * BLOCK * width),
            transcendentals=pairs,
        ),
    )(
        home_rows,
        guest_rows,
        home_cluster.reshape(1, -1),
        guest_cluster.reshape(1, -1),
        pair_mask.transpose(1, 0, 2),
    )
    return (home_score.reshape(-1), guest_score.reshape(-1))


def solution(mesh):
    placed = (
        P(("dp", "cluster"), None),
        P(("dp", "cluster"), None),
        P(),
        P(),
        P(("dp", "cluster"), None, None),
    )
    return jax.shard_map(
        body,
        mesh=mesh,
        in_specs=placed,
        out_specs=(P(("dp", "cluster")), P(("dp", "cluster"))),
        check_vma=False,
    )
```

```python
import functools

import jax
import jax.numpy as jnp
from jax import lax
from jax.experimental import pallas as pl
from jax.experimental.pallas import tpu as pltpu
from jax.sharding import PartitionSpec as P

BLOCK = 256
PARTS = 4
CHUNK = BLOCK // PARTS
BY_SIDE = 1

SHARPNESS = 30.0
EPSILON = 1e-06
MESH = pl.DeviceIdType.MESH


def lane_fold(value):
    return jnp.sum(value.reshape(value.shape[0] // 8, 8, value.shape[1]), axis=0)


def kernel(
    ndp, slots, home_ref, guest_ref, home_hbm, guest_hbm, mask_hbm, home_out, guest_out,
    rows, turned, blocks, inv_home, home_acc, col_parts, inbox, home_ids, guest_ids, mask,
    load_sem, own_sem, line_sem, side_sem, recv_sem, col_send, col_recv,
):
    d = lax.axis_index("dp")
    c = lax.axis_index("cluster")
    n_cluster = lax.axis_size("cluster")
    count = ndp // 2
    z = lax.div(d, 2)
    x = lax.rem(d, 2)
    mirror = c + 1 - 2 * lax.rem(c, 2)
    beside = d + 1 - 2 * x
    has_up = z < count - 1
    has_down = z > 0

    barrier = pltpu.get_barrier_semaphore()

    def greet(dp, cluster):
        pl.semaphore_signal(barrier, inc=1, device_id=(dp, cluster), device_id_type=MESH)

    greet(d, mirror)
    for column in (c, mirror):
        greet(beside, column)

        @pl.when(has_up)
        def _():
            greet(d + 2, column)

        @pl.when(has_down)
        def _():
            greet(d - 2, column)

    loads = [
        pltpu.make_async_copy(source, target, load_sem.at[i])
        for i, (source, target) in enumerate(
            ((home_ref, rows), (home_hbm, home_ids), (guest_hbm, guest_ids), (mask_hbm, mask))
        )
    ]
    for load in loads:
        load.start()

    pl.semaphore_wait(barrier, 3 + 2 * has_up.astype(jnp.int32) + 2 * has_down.astype(jnp.int32))

    def piece(part):
        return pl.ds(part * CHUNK, CHUNK)

    def own_copy(part, way, target):
        return pltpu.make_async_remote_copy(
            src_ref=guest_ref.at[piece(part), :],
            dst_ref=blocks.at[d, piece(part), :],
            send_sem=own_sem.at[way, part],
            recv_sem=recv_sem.at[d, part],
            device_id=(target, mirror),
            device_id_type=MESH,
        )

    def own_each(act, parts):
        for part in parts:

            @pl.when(has_up)
            def _():
                act(own_copy(part, 0, d + 2))

            @pl.when(has_down)
            def _():
                act(own_copy(part, 1, d - 2))

            act(own_copy(part, 2, beside))
            act(own_copy(part, 3, d))

    own_each(lambda copy: copy.start(), range(PARTS // 2))

    def passed(slot, part, sem, target):
        return pltpu.make_async_remote_copy(
            src_ref=blocks.at[slot, piece(part), :],
            dst_ref=blocks.at[slot, piece(part), :],
            send_sem=sem.at[slot, part],
            recv_sem=recv_sem.at[slot, part],
            device_id=(target, c),
            device_id_type=MESH,
        )

    def is_end(zz):
        return jnp.logical_or(zz == 0, zz == count - 1)

    def line_each(zz, part, act):
        slot = zz * 2 + x

        @pl.when(jnp.logical_and(has_up, zz < z))
        def _():
            act(passed(slot, part, line_sem, d + 2))

        @pl.when(jnp.logical_and(has_down, zz > z))
        def _():
            act(passed(slot, part, line_sem, d - 2))

        by_side = zz != z
        if part >= BY_SIDE:
            by_side = jnp.logical_and(by_side, jnp.logical_not(is_end(zz)))

        @pl.when(by_side)
        def _():
            act(passed(slot, part, side_sem, beside))

    def end_each(zz, part, act):
        slot = zz * 2 + 1 - x

        @pl.when(jnp.logical_and(has_up, zz == 0))
        def _():
            act(passed(slot, part, line_sem, d + 2))

        @pl.when(jnp.logical_and(has_down, zz == count - 1))
        def _():
            act(passed(slot, part, line_sem, d - 2))

    def col_copy(slot):
        return pltpu.make_async_remote_copy(
            src_ref=col_parts.at[slot],
            dst_ref=inbox.at[d],
            send_sem=col_send.at[slot],
            recv_sem=col_recv.at[d],
            device_id=(slot, mirror),
            device_id_type=MESH,
        )

    for load in loads:
        load.wait()

    def prepare(slot, carry):
        own = rows[pl.ds(pl.multiple_of(slot * BLOCK, BLOCK), BLOCK), :]
        flipped = own.T
        turned[slot] = flipped
        values = flipped.astype(jnp.float32)
        total = jnp.sum(lane_fold(values * values), axis=0, keepdims=True)
        scale = SHARPNESS * lax.rsqrt(total + EPSILON)
        inv_home[slot] = jnp.broadcast_to(scale, (8, BLOCK))
        home_acc[slot] = jnp.zeros((8, BLOCK), jnp.float32)
        return carry

    later = range(PARTS // 2, PARTS)
    done = 0
    for i, part in enumerate(later):
        upto = slots * (i + 1) // len(later)
        lax.fori_loop(done, upto, prepare, 0)
        done = upto
        own_each(lambda copy: copy.start(), (part,))

    def compute(slot, first, extent):
        visitor = blocks[slot, first : first + extent, :]
        values = visitor.astype(jnp.float32)
        inv = lax.rsqrt(jnp.sum(values * values, axis=1, keepdims=True) + EPSILON)
        inv = jnp.broadcast_to(inv, (extent, 128))
        guest_acc = jnp.zeros((extent, 128), jnp.float32)
        for s in range(slots):
            products = jnp.dot(visitor, turned[s], preferred_element_type=jnp.float32)
            listed = mask[s, 0, slot].astype(jnp.float32)
            both = jnp.zeros((extent, 128), jnp.float32)
            for lanes in (slice(0, 128), slice(128, 256)):
                tile = jnp.exp(products[:, lanes] * inv * inv_home[s, 0:1, lanes])
                home_acc[s, :, lanes] += lane_fold(tile) * listed
                both += tile
            guest_acc += both * listed
        col_parts[slot, :, first : first + extent] = lane_fold(guest_acc.T)

    def compute_all(slot):
        compute(slot, 0, BLOCK)
        col_copy(slot).start()

    def both_ways(dist, act):
        def way(plus, carry):
            zz = z + (2 * plus - 1) * dist
            valid = (dist >= 0) & (zz >= 0) & (zz < count)
            valid = valid & jnp.logical_not((dist == 0) & (plus == 1))

            @pl.when(valid)
            def _():
                act(zz)

            return carry

        lax.fori_loop(0, 2, way, 0)

    def arrive(zz, xx, part):
        passed(zz * 2 + xx, part, line_sem, d).wait_recv()

    def line_part(part):
        def act(zz):
            arrive(zz, x, part)
            line_each(zz, part, lambda copy: copy.start())

        return act

    def end_parts(zz):
        @pl.when(is_end(zz))
        def _():
            for part in range(BY_SIDE, PARTS):
                arrive(zz, 1 - x, part)
                end_each(zz, part, lambda copy: copy.start())

    def side_compute(zz):
        for part in range(BY_SIDE):
            arrive(zz, 1 - x, part)

        @pl.when(jnp.logical_not(is_end(zz)))
        def _():
            for part in range(BY_SIDE, PARTS):
                arrive(zz, 1 - x, part)

        compute_all(zz * 2 + 1 - x)

    def step(k, carry):
        for part in range(PARTS // 2):
            both_ways(k, line_part(part))
        both_ways(k - 2, side_compute)
        for part in range(PARTS // 2, PARTS):
            both_ways(k, line_part(part))
        both_ways(k, lambda zz: compute_all(zz * 2 + x))
        both_ways(k - 1, end_parts)
        return carry

    lax.fori_loop(0, count, step, 0)
    device = d * n_cluster + c
    home_list = home_ids[...]
    guest_list = guest_ids[...]

    def pick(ids, place):
        here = lax.broadcasted_iota(jnp.int32, ids.shape, 1) == place
        return jnp.sum(jnp.where(here, ids, 0), axis=1, keepdims=True)

    def log_members(own_id):
        number = jnp.sum((home_list == own_id).astype(jnp.int32), axis=1, keepdims=True)
        number += jnp.sum((guest_list == own_id).astype(jnp.int32), axis=1, keepdims=True)
        return jnp.log(number.astype(jnp.float32))

    log_home = [log_members(pick(home_list, device * slots + s)) for s in range(slots)]
    log_guest = log_members(pick(guest_list, device))

    both_ways(count - 2, side_compute)

    def far_compute(zz):
        slot = zz * 2 + 1 - x
        for half in range(2):
            for part in range(half * PARTS // 2, (half + 1) * PARTS // 2):
                arrive(zz, 1 - x, part)
            compute(slot, half * BLOCK // 2, BLOCK // 2)
        col_copy(slot).start()

    both_ways(count - 1, far_compute)

    for s in range(slots):
        density = jnp.sum(home_acc[s], axis=0, keepdims=True)
        score = jnp.log(1.0 + density) - log_home[s]
        home_out[:, s * BLOCK : (s + 1) * BLOCK] = score

    own_each(lambda copy: copy.wait_send(), range(PARTS))

    def drain(t, carry):
        for part in range(PARTS):
            line_each(t, part, lambda copy: copy.wait_send())
        for part in range(BY_SIDE, PARTS):
            end_each(t, part, lambda copy: copy.wait_send())
        return carry

    lax.fori_loop(0, count, drain, 0)

    def collect(t, total):
        pltpu.make_async_remote_copy(
            src_ref=col_parts.at[t],
            dst_ref=inbox.at[t],
            send_sem=col_send.at[t],
            recv_sem=col_recv.at[t],
            device_id=(t, mirror),
            device_id_type=MESH,
        ).wait_recv()
        return total + inbox[t]

    total = lax.fori_loop(0, ndp, collect, jnp.zeros((8, BLOCK), jnp.float32))
    guest_out[...] = jnp.log(1.0 + jnp.sum(total, axis=0, keepdims=True)) - log_guest

    def col_drain(t, carry):
        col_copy(t).wait_send()
        return carry

    lax.fori_loop(0, ndp, col_drain, 0)


def body(home_rows, guest_rows, home_cluster, guest_cluster, pair_mask):
    slots = home_rows.shape[0] // BLOCK
    width = home_rows.shape[1]
    ndp = lax.axis_size("dp")
    hbm = pl.BlockSpec(memory_space=pltpu.HBM)
    vmem = pl.BlockSpec(memory_space=pltpu.VMEM)
    pairs = slots * ndp * BLOCK * BLOCK
    home_score, guest_score = pl.pallas_call(
        functools.partial(kernel, ndp, slots),
        out_shape=(
            pltpu.VMEM((1, slots * BLOCK), jnp.float32),
            pltpu.VMEM((1, BLOCK), jnp.float32),
        ),
        in_specs=[hbm] * 5,
        out_specs=(vmem, vmem),
        scratch_shapes=[
            pltpu.VMEM((slots * BLOCK, width), jnp.bfloat16),
            pltpu.VMEM((slots, width, BLOCK), jnp.bfloat16),
            pltpu.VMEM((ndp, BLOCK, width), jnp.bfloat16),
            pltpu.VMEM((slots, 8, BLOCK), jnp.float32),
            pltpu.VMEM((slots, 8, BLOCK), jnp.float32),
            pltpu.VMEM((ndp, 8, BLOCK), jnp.float32),
            pltpu.VMEM((ndp, 8, BLOCK), jnp.float32),
            pltpu.VMEM((1, home_cluster.shape[0]), jnp.int32),
            pltpu.VMEM((1, guest_cluster.shape[0]), jnp.int32),
            pltpu.SMEM((slots, 1, ndp), jnp.int32),
            pltpu.SemaphoreType.DMA((4,)),
            pltpu.SemaphoreType.DMA((4, PARTS)),
            pltpu.SemaphoreType.DMA((ndp, PARTS)),
            pltpu.SemaphoreType.DMA((ndp, PARTS)),
            pltpu.SemaphoreType.DMA((ndp, PARTS)),
            pltpu.SemaphoreType.DMA((ndp,)),
            pltpu.SemaphoreType.DMA((ndp,)),
        ],
        compiler_params=pltpu.CompilerParams(
            collective_id=0, has_side_effects=True, vmem_limit_bytes=62 * 2**20
        ),
        cost_estimate=pl.CostEstimate(
            flops=2 * pairs * width,
            bytes_accessed=2 * (home_rows.size + ndp * BLOCK * width),
            transcendentals=pairs,
        ),
    )(
        home_rows,
        guest_rows,
        home_cluster.reshape(1, -1),
        guest_cluster.reshape(1, -1),
        pair_mask.transpose(1, 0, 2),
    )
    return (home_score.reshape(-1), guest_score.reshape(-1))


def solution(mesh):
    placed = (
        P(("dp", "cluster"), None),
        P(("dp", "cluster"), None),
        P(),
        P(),
        P(("dp", "cluster"), None, None),
    )
    return jax.shard_map(
        body,
        mesh=mesh,
        in_specs=placed,
        out_specs=(P(("dp", "cluster")), P(("dp", "cluster"))),
        check_vma=False,
    )
```

```python
import functools

import jax
import jax.numpy as jnp
from jax import lax
from jax.experimental import pallas as pl
from jax.experimental.pallas import tpu as pltpu
from jax.sharding import PartitionSpec as P

BLOCK = 256
PARTS = 4
CHUNK = BLOCK // PARTS
BY_SIDE = PARTS // 2

SHARPNESS = 30.0
EPSILON = 1e-06
MESH = pl.DeviceIdType.MESH


def lane_fold(value):
    return jnp.sum(value.reshape(value.shape[0] // 8, 8, value.shape[1]), axis=0)


def kernel(
    ndp, slots, home_ref, guest_ref, home_hbm, guest_hbm, mask_hbm, home_out, guest_out,
    rows, turned, blocks, inv_home, home_acc, col_parts, inbox, home_ids, guest_ids, mask,
    load_sem, own_sem, line_sem, side_sem, recv_sem, col_send, col_recv,
):
    d = lax.axis_index("dp")
    c = lax.axis_index("cluster")
    n_cluster = lax.axis_size("cluster")
    count = ndp // 2
    z = lax.div(d, 2)
    x = lax.rem(d, 2)
    mirror = c + 1 - 2 * lax.rem(c, 2)
    beside = d + 1 - 2 * x
    has_up = z < count - 1
    has_down = z > 0

    barrier = pltpu.get_barrier_semaphore()

    def greet(dp, cluster):
        pl.semaphore_signal(barrier, inc=1, device_id=(dp, cluster), device_id_type=MESH)

    greet(d, mirror)
    for column in (c, mirror):
        greet(beside, column)

        @pl.when(has_up)
        def _():
            greet(d + 2, column)

        @pl.when(has_down)
        def _():
            greet(d - 2, column)

    loads = [
        pltpu.make_async_copy(source, target, load_sem.at[i])
        for i, (source, target) in enumerate(
            ((home_ref, rows), (home_hbm, home_ids), (guest_hbm, guest_ids), (mask_hbm, mask))
        )
    ]
    for load in loads:
        load.start()

    pl.semaphore_wait(barrier, 3 + 2 * has_up.astype(jnp.int32) + 2 * has_down.astype(jnp.int32))

    def piece(part):
        return pl.ds(part * CHUNK, CHUNK)

    def own_copy(part, way, target):
        return pltpu.make_async_remote_copy(
            src_ref=guest_ref.at[piece(part), :],
            dst_ref=blocks.at[d, piece(part), :],
            send_sem=own_sem.at[way, part],
            recv_sem=recv_sem.at[d, part],
            device_id=(target, mirror),
            device_id_type=MESH,
        )

    def own_each(act, parts):
        for part in parts:

            @pl.when(has_up)
            def _():
                act(own_copy(part, 0, d + 2))

            @pl.when(has_down)
            def _():
                act(own_copy(part, 1, d - 2))

            act(own_copy(part, 2, beside))
            act(own_copy(part, 3, d))

    own_each(lambda copy: copy.start(), range(PARTS // 2))

    def passed(slot, part, sem, target):
        return pltpu.make_async_remote_copy(
            src_ref=blocks.at[slot, piece(part), :],
            dst_ref=blocks.at[slot, piece(part), :],
            send_sem=sem.at[slot, part],
            recv_sem=recv_sem.at[slot, part],
            device_id=(target, c),
            device_id_type=MESH,
        )

    def is_end(zz):
        return jnp.logical_or(zz == 0, zz == count - 1)

    def line_each(zz, part, act):
        slot = zz * 2 + x

        @pl.when(jnp.logical_and(has_up, zz < z))
        def _():
            act(passed(slot, part, line_sem, d + 2))

        @pl.when(jnp.logical_and(has_down, zz > z))
        def _():
            act(passed(slot, part, line_sem, d - 2))

        by_side = zz != z
        if part >= BY_SIDE:
            by_side = jnp.logical_and(by_side, jnp.logical_not(is_end(zz)))

        @pl.when(by_side)
        def _():
            act(passed(slot, part, side_sem, beside))

    def end_each(zz, part, act):
        slot = zz * 2 + 1 - x

        @pl.when(jnp.logical_and(has_up, zz == 0))
        def _():
            act(passed(slot, part, line_sem, d + 2))

        @pl.when(jnp.logical_and(has_down, zz == count - 1))
        def _():
            act(passed(slot, part, line_sem, d - 2))

    def col_copy(slot):
        return pltpu.make_async_remote_copy(
            src_ref=col_parts.at[slot],
            dst_ref=inbox.at[d],
            send_sem=col_send.at[slot],
            recv_sem=col_recv.at[d],
            device_id=(slot, mirror),
            device_id_type=MESH,
        )

    for load in loads:
        load.wait()

    def prepare(slot, carry):
        own = rows[pl.ds(pl.multiple_of(slot * BLOCK, BLOCK), BLOCK), :]
        flipped = own.T
        turned[slot] = flipped
        values = flipped.astype(jnp.float32)
        total = jnp.sum(lane_fold(values * values), axis=0, keepdims=True)
        scale = SHARPNESS * lax.rsqrt(total + EPSILON)
        inv_home[slot] = jnp.broadcast_to(scale, (8, BLOCK))
        home_acc[slot] = jnp.zeros((8, BLOCK), jnp.float32)
        return carry

    lax.fori_loop(0, slots // 2, prepare, 0)
    own_each(lambda copy: copy.start(), range(PARTS // 2, PARTS))
    lax.fori_loop(slots // 2, slots, prepare, 0)

    def compute(slot, first, extent):
        visitor = blocks[slot, first : first + extent, :]
        values = visitor.astype(jnp.float32)
        inv = lax.rsqrt(jnp.sum(values * values, axis=1, keepdims=True) + EPSILON)
        inv = jnp.broadcast_to(inv, (extent, 128))
        guest_acc = jnp.zeros((extent, 128), jnp.float32)
        for s in range(slots):
            products = jnp.dot(visitor, turned[s], preferred_element_type=jnp.float32)
            listed = mask[s, 0, slot].astype(jnp.float32)
            both = jnp.zeros((extent, 128), jnp.float32)
            for lanes in (slice(0, 128), slice(128, 256)):
                tile = jnp.exp(products[:, lanes] * inv * inv_home[s, 0:1, lanes])
                home_acc[s, :, lanes] += lane_fold(tile) * listed
                both += tile
            guest_acc += both * listed
        col_parts[slot, :, first : first + extent] = lane_fold(guest_acc.T)

    def compute_all(slot):
        compute(slot, 0, BLOCK)
        col_copy(slot).start()

    def both_ways(dist, act):
        def way(plus, carry):
            zz = z + (2 * plus - 1) * dist
            valid = (dist >= 0) & (zz >= 0) & (zz < count)
            valid = valid & jnp.logical_not((dist == 0) & (plus == 1))

            @pl.when(valid)
            def _():
                act(zz)

            return carry

        lax.fori_loop(0, 2, way, 0)

    def arrive(zz, xx, part):
        passed(zz * 2 + xx, part, line_sem, d).wait_recv()

    def line_part(part):
        def act(zz):
            arrive(zz, x, part)
            line_each(zz, part, lambda copy: copy.start())

        return act

    def end_parts(zz):
        @pl.when(is_end(zz))
        def _():
            for part in range(BY_SIDE, PARTS):
                arrive(zz, 1 - x, part)
                end_each(zz, part, lambda copy: copy.start())

    def side_compute(zz):
        for part in range(BY_SIDE):
            arrive(zz, 1 - x, part)

        @pl.when(jnp.logical_not(is_end(zz)))
        def _():
            for part in range(BY_SIDE, PARTS):
                arrive(zz, 1 - x, part)

        compute_all(zz * 2 + 1 - x)

    def step(k, carry):
        for part in range(PARTS // 2):
            both_ways(jnp.where(k > 1, k, -1), line_part(part))
        both_ways(jnp.where(k > 1, k - 1, -1), end_parts)
        both_ways(k - 2, side_compute)
        for part in range(PARTS // 2, PARTS):
            both_ways(k, line_part(part))
        both_ways(jnp.where(k == 1, 0, -1), end_parts)
        both_ways(k, lambda zz: compute_all(zz * 2 + x))
        return carry

    for part in range(PARTS // 2):
        both_ways(1, line_part(part))
    for part in range(PARTS):
        arrive(z, x, part)
    compute_all(d)
    lax.fori_loop(1, count, step, 0)

    device = d * n_cluster + c
    home_list = home_ids[...]
    guest_list = guest_ids[...]

    def pick(ids, place):
        here = lax.broadcasted_iota(jnp.int32, ids.shape, 1) == place
        return jnp.sum(jnp.where(here, ids, 0), axis=1, keepdims=True)

    def log_members(own_id):
        number = jnp.sum((home_list == own_id).astype(jnp.int32), axis=1, keepdims=True)
        number += jnp.sum((guest_list == own_id).astype(jnp.int32), axis=1, keepdims=True)
        return jnp.log(number.astype(jnp.float32))

    log_home = [log_members(pick(home_list, device * slots + s)) for s in range(slots)]
    log_guest = log_members(pick(guest_list, device))

    both_ways(count - 2, side_compute)

    def far_compute(zz):
        slot = zz * 2 + 1 - x
        for half in range(2):
            for part in range(half * PARTS // 2, (half + 1) * PARTS // 2):
                arrive(zz, 1 - x, part)
            compute(slot, half * BLOCK // 2, BLOCK // 2)
        col_copy(slot).start()

    both_ways(count - 1, far_compute)

    for s in range(slots):
        density = jnp.sum(home_acc[s], axis=0, keepdims=True)
        score = jnp.log(1.0 + density) - log_home[s]
        home_out[:, s * BLOCK : (s + 1) * BLOCK] = score

    own_each(lambda copy: copy.wait_send(), range(PARTS))

    def drain(t, carry):
        for part in range(PARTS):
            line_each(t, part, lambda copy: copy.wait_send())
        for part in range(BY_SIDE, PARTS):
            end_each(t, part, lambda copy: copy.wait_send())
        return carry

    lax.fori_loop(0, count, drain, 0)

    def collect(t, total):
        pltpu.make_async_remote_copy(
            src_ref=col_parts.at[t],
            dst_ref=inbox.at[t],
            send_sem=col_send.at[t],
            recv_sem=col_recv.at[t],
            device_id=(t, mirror),
            device_id_type=MESH,
        ).wait_recv()
        return total + inbox[t]

    total = lax.fori_loop(0, ndp, collect, jnp.zeros((8, BLOCK), jnp.float32))
    guest_out[...] = jnp.log(1.0 + jnp.sum(total, axis=0, keepdims=True)) - log_guest

    def col_drain(t, carry):
        col_copy(t).wait_send()
        return carry

    lax.fori_loop(0, ndp, col_drain, 0)


def body(home_rows, guest_rows, home_cluster, guest_cluster, pair_mask):
    slots = home_rows.shape[0] // BLOCK
    width = home_rows.shape[1]
    ndp = lax.axis_size("dp")
    hbm = pl.BlockSpec(memory_space=pltpu.HBM)
    vmem = pl.BlockSpec(memory_space=pltpu.VMEM)
    pairs = slots * ndp * BLOCK * BLOCK
    home_score, guest_score = pl.pallas_call(
        functools.partial(kernel, ndp, slots),
        out_shape=(
            pltpu.VMEM((1, slots * BLOCK), jnp.float32),
            pltpu.VMEM((1, BLOCK), jnp.float32),
        ),
        in_specs=[hbm] * 5,
        out_specs=(vmem, vmem),
        scratch_shapes=[
            pltpu.VMEM((slots * BLOCK, width), jnp.bfloat16),
            pltpu.VMEM((slots, width, BLOCK), jnp.bfloat16),
            pltpu.VMEM((ndp, BLOCK, width), jnp.bfloat16),
            pltpu.VMEM((slots, 8, BLOCK), jnp.float32),
            pltpu.VMEM((slots, 8, BLOCK), jnp.float32),
            pltpu.VMEM((ndp, 8, BLOCK), jnp.float32),
            pltpu.VMEM((ndp, 8, BLOCK), jnp.float32),
            pltpu.VMEM((1, home_cluster.shape[0]), jnp.int32),
            pltpu.VMEM((1, guest_cluster.shape[0]), jnp.int32),
            pltpu.SMEM((slots, 1, ndp), jnp.int32),
            pltpu.SemaphoreType.DMA((4,)),
            pltpu.SemaphoreType.DMA((4, PARTS)),
            pltpu.SemaphoreType.DMA((ndp, PARTS)),
            pltpu.SemaphoreType.DMA((ndp, PARTS)),
            pltpu.SemaphoreType.DMA((ndp, PARTS)),
            pltpu.SemaphoreType.DMA((ndp,)),
            pltpu.SemaphoreType.DMA((ndp,)),
        ],
        compiler_params=pltpu.CompilerParams(
            collective_id=0, has_side_effects=True, vmem_limit_bytes=62 * 2**20
        ),
        cost_estimate=pl.CostEstimate(
            flops=2 * pairs * width,
            bytes_accessed=2 * (home_rows.size + ndp * BLOCK * width),
            transcendentals=pairs,
        ),
    )(
        home_rows,
        guest_rows,
        home_cluster.reshape(1, -1),
        guest_cluster.reshape(1, -1),
        pair_mask.transpose(1, 0, 2),
    )
    return (home_score.reshape(-1), guest_score.reshape(-1))


def solution(mesh):
    placed = (
        P(("dp", "cluster"), None),
        P(("dp", "cluster"), None),
        P(),
        P(),
        P(("dp", "cluster"), None, None),
    )
    return jax.shard_map(
        body,
        mesh=mesh,
        in_specs=placed,
        out_specs=(P(("dp", "cluster")), P(("dp", "cluster"))),
        check_vma=False,
    )
```
